32 devices in a mesh: groups: 2 (over y), dev: 8 (over z, x), pair: 2 (over core).
Axes of the slice: x: 2, y: 2, z: 4, core: 2. Of those that a mesh axis runs over, the one named last changes fastest.
Arguments:
- query: bfloat16 [512, 64, 128], P(('groups', 'dev', 'pair')), parts along dimension 0, may hold values from -10 to 10
- stored_keys: bfloat16 [512, 256, 4, 128], P(('groups', 'dev', 'pair')), parts along dimension 0, may hold values from -30 to 30
- stored_values: bfloat16 [512, 256, 4, 128], P(('groups', 'dev', 'pair')), parts along dimension 0, may hold values from -6 to 6
- incoming_key: bfloat16 [512, 4, 128], P(('groups', 'dev', 'pair')), parts along dimension 0, may hold values from -6 to 6
- incoming_value: bfloat16 [512, 4, 128], P(('groups', 'dev', 'pair')), parts along dimension 0, may hold values from -6 to 6
- lengths: int32 [512], P(('groups', 'dev', 'pair')), parts along dimension 0, may hold values from 2 to 256, as said below
- out_weight: bfloat16 [8192, 2048], P('dev', 'pair'), may hold values from -0.25 to 0.25
- residual: bfloat16 [512, 2048], P(('groups', 'dev'), 'pair'), parts along dimension 0, may hold values from -6 to 6
- norm_gain: float32 [2048], P('pair'), may hold values from 0.1 to 1.9
- expert_ids: int32 [512, 8], P(('groups', 'dev')), parts along dimension 0, may hold values from 0 to 15, all different within a row; in each aligned block of 32 rows (0 to 31, 32 to 63, ...) at most 24 rows name the same one
- route_weights: float32 [512, 8], P(('groups', 'dev')), parts along dimension 0, may hold values from 0.05 to 1
- w_gate: bfloat16 [16, 2048, 768], P('dev', 'pair'), may hold values from -0.125 to 0.125
- w_up: bfloat16 [16, 2048, 768], P('dev', 'pair'), may hold values from -0.125 to 0.125
- w_down: bfloat16 [16, 768, 2048], P('dev', None, 'pair'), may hold values from -0.4375 to 0.4375
Outputs:
- layer_out: bfloat16 [512, 2048], P(('groups', 'dev'), 'pair'), parts along dimension 0
The draws below stay inside these ranges and needn't reach their ends.
There are 2 independent parts, one for each index of `groups`. The reference program is written for one: setup_inputs(seed, part) draws one part's arguments, and reference() takes and returns one part's arrays. A program takes and returns all parts, laid end to end along the dimension named above; an argument that names none is the same for every part. Nothing has to cross between parts.
Inputs may be any that keep to these rules, and one draw needn't show every extreme that they name: `lengths`: every draw has a row with exactly 256 valid positions. `expert_ids`: each row names 8 different experts; among the rows of one index of dev no expert is named by more than 24 rows.
All inputs are finite; a program needn't handle non-finite values.
Results may differ from the reference program's by a relative error of at most 0.0085.
Values may be sent and summed in bfloat16 or wider, within the bound.
No kernel may reach another device: no remote copies, remote signals or barrier semaphores. Data moves between devices by JAX's collectives and lax.ppermute only.
A program may use at most 128 MiB of HBM per device.

```python
import math
import jax
import jax.numpy as jnp
import numpy as np
from jax import lax

D = 2048
QUERY_HEADS = 64
KEY_VALUE_HEADS = 4
HEAD_DIMENSION = 128
EFF = 768
TOPK = 8
TOKEN_ROWS_SHARD = 32
CACHE_LENGTH = 256
EXPERTS = 16
DECODE_ROWS = 256
CAP = 24
N_DEV = 8


def draw_query(key, part):
    key = jax.random.fold_in(key, 11)
    random_jitter = jnp.clip(jax.random.normal(key, (DECODE_ROWS, QUERY_HEADS, HEAD_DIMENSION), jnp.float32), -6.0, 6.0)
    return random_jitter.astype(jnp.bfloat16)


def draw_stored_keys(key, part):
    key = jax.random.fold_in(key, 12)
    random_jitter = jnp.clip(jax.random.normal(key, (DECODE_ROWS, CACHE_LENGTH, KEY_VALUE_HEADS, HEAD_DIMENSION), jnp.float32), -6.0, 6.0)
    return random_jitter.astype(jnp.bfloat16)


def draw_lengths(key, part):
    key = jax.random.fold_in(key, 13)
    initial_random_key, latter_random_key = jax.random.split(key)
    drawn = jax.random.randint(initial_random_key, (DECODE_ROWS,), 2, CACHE_LENGTH + 1, jnp.int32)
    chosen = jax.random.randint(latter_random_key, (), 0, DECODE_ROWS, jnp.int32)
    return jnp.where(jnp.arange(DECODE_ROWS, dtype=jnp.int32) == chosen, CACHE_LENGTH, drawn).astype(jnp.int32)


def level_of(stream_key, dims, pieces, least, top_value):
    def one(axis_at, blocks):
        heights = jax.random.uniform(jax.random.fold_in(jax.random.fold_in(stream_key, 6), axis_at), (blocks,), jnp.float32, least / len(pieces), top_value / len(pieces))
        return jnp.repeat(jnp.exp(heights), dims[axis_at] // blocks).reshape((-1,) + (1,) * (len(dims) - axis_at - 1))

    loudness = one(*pieces[0])
    for cut in pieces[1:]:
        loudness = loudness * one(*cut)
    return loudness


def assign_block(key, own, number, rows, number_of, top, most, skew):
    ranking = jax.random.permutation(key, number_of)
    crowded, usual = portions_of(number_of, rows * top, most, skew, True), portions_of(number_of, rows * top, most, skew, False)
    places = jnp.arange(number_of)

    def named(sizes, offset_by):
        used = int((sizes > 0).sum())
        fixed = max(1, used // 4)
        moved = fixed + (places - fixed + offset_by * (used - fixed)) % max(1, number_of - fixed)
        return jnp.zeros((number_of,), jnp.int32).at[ranking[jnp.where(places < fixed, places, moved)]].set(jnp.asarray(sizes, jnp.int32))

    sizes = jnp.where(number % 4 == 0, named(crowded, number // 4), named(usual, number - number // 4 - 1))
    mixed = jax.random.permutation(jax.random.fold_in(own, 3), number_of)
    source_of, receiver = mixed[0:number_of // 2 * 2:2], mixed[1:number_of // 2 * 2:2]
    slack = jnp.minimum(sizes[source_of] - 1, most - sizes[receiver]) // 2
    slack = jnp.where((source_of == ranking[0]) | (receiver == ranking[0]) | (sizes[receiver] == 0), 0, jnp.maximum(slack, 0))
    moved = jax.random.randint(jax.random.fold_in(own, 4), (number_of // 2,), 0, 1 << 20) % (slack + 1)
    sizes = sizes.at[source_of].add(-moved).at[receiver].add(moved)
    items = jnp.searchsorted(jnp.cumsum(sizes), jnp.arange(rows * top), side="right").astype(jnp.int32)
    grid = items.reshape(top, rows).T
    grid = grid[jax.random.permutation(jax.random.fold_in(own, 1), rows)]
    offset_by = jax.random.randint(jax.random.fold_in(own, 2), (rows, 1), 0, top)
    return jnp.take_along_axis(grid, (jnp.arange(top)[None, :] + offset_by) % top, axis=1)


def portions_of(amount, total, limit, lean, full):
    weights = [(1 << 20) // math.isqrt(rank ** lean) + 1 for rank in range(1, amount + 1)]
    largest = limit if full else min(limit, max(-(-total // amount), total * weights[0] // sum(weights)))
    least = 1 if total - largest >= amount - 1 else 0
    holding, surplus = [largest] + [least] * (amount - 1), total - largest - least * (amount - 1)
    while surplus > 0:
        candidates = [i for i in range(1, amount) if holding[i] < largest] or [i for i in range(1, amount) if holding[i] < limit]
        whole, remaining = sum([weights[i] for i in candidates]), surplus
        for i in candidates:
            addition = min(limit - holding[i], max(1, remaining * weights[i] // whole), surplus)
            holding[i] = holding[i] + addition
            surplus = surplus - addition
    return np.array(holding)


def gaussian(stream_key, shape, scale, limit, cuts=(), kind=jnp.bfloat16):
    array = scale * jax.random.normal(stream_key, shape, jnp.float32)
    if cuts:
        array = array * level_of(stream_key, shape, cuts, -0.22, 0.18)
    return jnp.clip(array, -limit, limit).astype(kind)


def setup_inputs(seed: int = 0, part: int = 0) -> dict:
    streams_of = jax.random.split(jax.random.key(seed), 15)
    own_keys = jax.random.split(jax.random.fold_in(streams_of[14], part), 15)
    query = draw_query(jax.random.fold_in(jax.random.fold_in(streams_of[14], part), 71), part)
    stored_keys = draw_stored_keys(jax.random.fold_in(jax.random.fold_in(streams_of[14], part), 71), part)
    stored_values = gaussian(own_keys[2], (DECODE_ROWS, CACHE_LENGTH, KEY_VALUE_HEADS, HEAD_DIMENSION), 1.0, 6.0, ((0, 16),))
    incoming_key = gaussian(own_keys[3], (DECODE_ROWS, KEY_VALUE_HEADS, HEAD_DIMENSION), 1.0, 6.0, ((0, 16),))
    incoming_value = gaussian(own_keys[4], (DECODE_ROWS, KEY_VALUE_HEADS, HEAD_DIMENSION), 1.0, 6.0, ((0, 16),))
    lengths = draw_lengths(jax.random.fold_in(jax.random.fold_in(streams_of[14], part), 71), part)
    out_weight = gaussian(streams_of[6], (QUERY_HEADS * HEAD_DIMENSION, D), (QUERY_HEADS * HEAD_DIMENSION // 16) ** -0.5, 0.25, ((0, 8), (1, 2)))
    residual = gaussian(own_keys[7], (DECODE_ROWS, D), 1.0, 6.0, ((0, 8), (1, 2)))
    norm_gain = jnp.clip(1.0 + 0.18 * jax.random.normal(streams_of[8], (D,), jnp.float32), 0.1, 1.9)
    expert_ids_keys = jax.random.split(jax.random.fold_in(own_keys[9], 1), DECODE_ROWS // TOKEN_ROWS_SHARD)
    expert_ids_turns = jax.random.permutation(jax.random.fold_in(own_keys[9], 3), DECODE_ROWS // TOKEN_ROWS_SHARD)
    expert_ids = jax.vmap(lambda own, number: assign_block(jax.random.fold_in(own_keys[9], 2), own, number, TOKEN_ROWS_SHARD, EXPERTS, TOPK, CAP, 2))(expert_ids_keys, expert_ids_turns).reshape((DECODE_ROWS, TOPK))
    route_weights = jnp.clip(jnp.exp(math.log(1.0) - 2.9957323 * jax.random.uniform(own_keys[10], (DECODE_ROWS, TOPK), jnp.float32) ** level_of(own_keys[10], (DECODE_ROWS, TOPK), ((0, 8),), -0.2, 0.2)), 0.05, 1.0)
    w_gate = gaussian(streams_of[11], (EXPERTS, D, EFF), D ** -0.5, 0.125, ((0, 8), (1, 2)))
    w_up = gaussian(streams_of[12], (EXPERTS, D, EFF), D ** -0.5, 0.125, ((0, 8), (1, 2)))
    w_down = gaussian(streams_of[13], (EXPERTS, EFF, D), (EFF // 4) ** -0.5, 0.4375, ((0, 8), (2, 2)))
    return dict(query=query, stored_keys=stored_keys, stored_values=stored_values, incoming_key=incoming_key, incoming_value=incoming_value, lengths=lengths, out_weight=out_weight, residual=residual, norm_gain=norm_gain, expert_ids=expert_ids, route_weights=route_weights, w_gate=w_gate, w_up=w_up, w_down=w_down)


def attend(block):
    query, keys, vals, fresh_key, fresh_val, lens = block
    high = lax.Precision.HIGHEST
    grouped_queries = query.astype(jnp.float32).reshape(-1, KEY_VALUE_HEADS, QUERY_HEADS // KEY_VALUE_HEADS, HEAD_DIMENSION)
    factor = HEAD_DIMENSION ** (-0.5)
    scores = jnp.einsum('bgjd,btgd->bgjt', grouped_queries, keys.astype(jnp.float32), precision=high) * factor
    valid = (jnp.arange(CACHE_LENGTH, dtype=jnp.int32)[None, :] < lens[:, None])[:, None, None, :]
    scores = jnp.where(valid, scores, -1e+30)
    own = jnp.einsum('bgjd,bgd->bgj', grouped_queries, fresh_key.astype(jnp.float32), precision=high) * factor
    peak = jnp.maximum(lax.optimization_barrier(jnp.max(scores, axis=3)), own)
    expo = jnp.where(valid, jnp.exp(scores - peak[..., None]), 0.0)
    own_expo = jnp.exp(own - peak)
    total = lax.optimization_barrier(jnp.sum(expo, axis=3)) + own_expo
    accum = jnp.einsum('bgjt,btgd->bgjd', expo, vals.astype(jnp.float32), precision=high)
    accum = accum + own_expo[..., None] * fresh_val.astype(jnp.float32)[:, :, None, :]
    return (accum / total[..., None]).reshape(-1, QUERY_HEADS * HEAD_DIMENSION).astype(jnp.bfloat16)

def run_expert(block):
    rows_in, gate_w, up_w, down_w = block
    gate = jnp.dot(rows_in, gate_w, preferred_element_type=jnp.float32)
    up = jnp.dot(rows_in, up_w, preferred_element_type=jnp.float32)
    active = (jax.nn.silu(gate) * up).astype(jnp.bfloat16)
    return jnp.dot(active, down_w, preferred_element_type=jnp.float32).astype(jnp.bfloat16)

def reference(query, stored_keys, stored_values, incoming_key, incoming_value, lengths, out_weight, residual, norm_gain, expert_ids, route_weights, w_gate, w_up, w_down):
    block_list = (query.reshape(N_DEV, TOKEN_ROWS_SHARD, QUERY_HEADS, HEAD_DIMENSION), stored_keys.reshape(N_DEV, TOKEN_ROWS_SHARD, CACHE_LENGTH, KEY_VALUE_HEADS, HEAD_DIMENSION), stored_values.reshape(N_DEV, TOKEN_ROWS_SHARD, CACHE_LENGTH, KEY_VALUE_HEADS, HEAD_DIMENSION), incoming_key.reshape(N_DEV, TOKEN_ROWS_SHARD, KEY_VALUE_HEADS, HEAD_DIMENSION), incoming_value.reshape(N_DEV, TOKEN_ROWS_SHARD, KEY_VALUE_HEADS, HEAD_DIMENSION), lengths.reshape(N_DEV, TOKEN_ROWS_SHARD))
    attended = lax.map(attend, block_list).reshape(DECODE_ROWS, QUERY_HEADS * HEAD_DIMENSION)
    mixed = residual.astype(jnp.float32) + jnp.dot(attended, out_weight, preferred_element_type=jnp.float32)
    mean_sq = lax.optimization_barrier(jnp.mean(mixed * mixed, axis=1, keepdims=True))
    normed = (mixed * lax.rsqrt(mean_sq + 1e-06) * norm_gain[None, :]).astype(jnp.bfloat16)
    per_expert = N_DEV * CAP
    flat_ids = expert_ids.reshape(-1).astype(jnp.int32)
    onehot = (flat_ids[:, None] == jnp.arange(EXPERTS, dtype=jnp.int32)[None, :]).astype(jnp.int32)
    rank = lax.optimization_barrier(jnp.sum((jnp.cumsum(onehot, axis=0) - onehot) * onehot, axis=1)).astype(jnp.int32)
    slot = (flat_ids * per_expert + rank).astype(jnp.int32)
    source = (jnp.arange(DECODE_ROWS * TOPK, dtype=jnp.int32) // TOPK).astype(jnp.int32)
    table = jnp.zeros((EXPERTS * per_expert,), jnp.int32).at[slot].set(source)
    buffer = normed[table].reshape(EXPERTS, per_expert, D)
    produced = lax.map(run_expert, (buffer, w_gate, w_up, w_down)).reshape(EXPERTS * per_expert, D)
    picked = produced[slot].reshape(DECODE_ROWS, TOPK, D).astype(jnp.float32)
    shares = route_weights / lax.optimization_barrier(jnp.sum(route_weights, axis=1, keepdims=True))
    result = mixed + lax.optimization_barrier(jnp.sum(shares[:, :, None] * picked, axis=1))
    return result.astype(jnp.bfloat16)
```

```python
import functools

import jax
import jax.numpy as jnp
from jax import lax
from jax.experimental import pallas as pl
from jax.experimental.pallas import tpu as pltpu
from jax.sharding import PartitionSpec as P

F32 = jnp.float32
BF16 = jnp.bfloat16


def attend_kernel(kv_heads, len_ref, q_ref, k_ref, v_ref, ik_ref, iv_ref, o_ref):
    block_rows, heads, size = q_ref.shape
    span = k_ref.shape[1]
    per = heads // kv_heads
    factor = size ** (-0.5)
    base = pl.program_id(0) * block_rows
    column = lax.broadcasted_iota(jnp.int32, (heads, span), 1)
    head = lax.broadcasted_iota(jnp.int32, (heads, span), 0)
    same = lax.rem(column, kv_heads) == head // per
    for i in range(block_rows):
        q = q_ref[i]
        scores = lax.dot_general(
            q, k_ref[i], (((1,), (1,)), ((), ())), preferred_element_type=F32
        )
        valid = same & (column < len_ref[base + i] * kv_heads)
        masked = jnp.where(valid, scores * factor, -1e30)
        spread = lambda ref: jnp.concatenate(
            [jnp.broadcast_to(ref[i, g : g + 1, :].astype(F32), (per, size)) for g in range(kv_heads)], axis=0
        )
        own = jnp.sum(q.astype(F32) * spread(ik_ref), axis=1, keepdims=True) * factor
        peak = jnp.maximum(jnp.max(masked, axis=1, keepdims=True), own)
        expo = jnp.exp(masked - peak)
        fresh = jnp.exp(own - peak)
        total = jnp.sum(expo, axis=1, keepdims=True) + fresh
        accum = jnp.dot(expo.astype(BF16), v_ref[i], preferred_element_type=F32)
        accum = accum + fresh * spread(iv_ref)
        o_ref[i] = (accum / total).astype(o_ref.dtype)


def attend(query, keys, values, fresh_key, fresh_value, lengths):
    rows, heads, size = query.shape
    positions, kv_heads = keys.shape[1:3]
    span = positions * kv_heads
    block = 2
    at = lambda i, _: (i, 0, 0)
    grid_spec = pltpu.PrefetchScalarGridSpec(
        num_scalar_prefetch=1,
        grid=(rows // block,),
        in_specs=[
            pl.BlockSpec((block, heads, size), at),
            pl.BlockSpec((block, span, size), at),
            pl.BlockSpec((block, span, size), at),
            pl.BlockSpec((block, kv_heads, size), at),
            pl.BlockSpec((block, kv_heads, size), at),
        ],
        out_specs=pl.BlockSpec((block, heads, size), at),
    )
    return pl.pallas_call(
        functools.partial(attend_kernel, kv_heads),
        out_shape=jax.ShapeDtypeStruct(query.shape, BF16),
        grid_spec=grid_spec,
        compiler_params=pltpu.CompilerParams(vmem_limit_bytes=32 * 1024 * 1024),
    )(
        lengths,
        query,
        keys.reshape(rows, span, size),
        values.reshape(rows, span, size),
        fresh_key,
        fresh_value,
    )


def per_device(
    query,
    stored_keys,
    stored_values,
    incoming_key,
    incoming_value,
    lengths,
    out_weight,
    residual,
    norm_gain,
    expert_ids,
    route_weights,
    w_gate,
    w_up,
    w_down,
):
    devs = lax.axis_size("dev")
    cores = lax.axis_size("pair")
    me = lax.axis_index("dev")
    core = lax.axis_index("pair")
    slots = devs // cores
    offset = [[c * slots + s for s in range(slots)] for c in range(cores)]

    def from_core(value, m):
        return lax.ppermute(value, "pair", [(c, c ^ m) for c in range(cores)])

    def swap(value, s):
        pairs = [
            (d * cores + c, (d ^ offset[c][s]) * cores + c)
            for d in range(devs)
            for c in range(cores)
            if offset[c][s]
        ]
        moved = lax.ppermute(value, ("dev", "pair"), pairs)
        if any(offset[c][s] == 0 for c in range(cores)):
            keep = functools.reduce(
                jnp.logical_or, [core == c for c in range(cores) if offset[c][s] == 0]
            )
            moved = jnp.where(keep, value, moved)
        return moved

    def gathered(value):
        return [value] + [from_core(value, m) for m in range(1, cores)]

    rows, part = residual.shape
    width = part * cores
    wo = gathered(out_weight)
    wg = gathered(w_gate)
    wu = gathered(w_up)
    wd = gathered(w_down)
    stream = jnp.concatenate(gathered(residual), axis=1).astype(F32)
    gain = jnp.concatenate(gathered(norm_gain), axis=0)

    attended = attend(query, stored_keys, stored_values, incoming_key, incoming_value, lengths)
    local_rows = query.shape[0]
    features = out_weight.shape[0]
    attended = attended.reshape(local_rows, devs, features)
    places = jnp.array(offset, dtype=jnp.int32) ^ me

    def blocks_of(c):
        return jnp.take(attended, places[c], axis=1)

    held = [blocks_of(core)]
    for m in range(1, cores):
        held.append(from_core(blocks_of(core ^ m), m))
    stacked = jnp.stack(held, axis=0)
    stacked = jnp.take(stacked, jnp.arange(cores, dtype=jnp.int32) ^ core, axis=0)
    stacked = stacked.reshape(rows, slots, features)
    arrived = jnp.concatenate([swap(stacked[:, s], s) for s in range(slots)], axis=0)
    partial = jnp.concatenate(
        [jnp.dot(arrived, w, preferred_element_type=F32) for w in wo], axis=1
    ).astype(BF16)
    sums = sum(
        swap(partial[s * rows : (s + 1) * rows], s).astype(F32) for s in range(slots)
    )

    def other_order(value, m):
        pieces = [value[:, j * part : (j + 1) * part] for j in range(cores)]
        return jnp.concatenate([pieces[j ^ m] for j in range(cores)], axis=1)

    mixed = stream + sums
    for m in range(1, cores):
        mixed = mixed + other_order(from_core(sums, m), m)
    squares = jnp.sum(mixed * mixed, axis=1, keepdims=True)
    normed = (mixed * lax.rsqrt(squares / width + 1e-06) * gain[None, :]).astype(BF16)

    local_experts = w_gate.shape[0]
    experts = local_experts * devs
    shares = route_weights / jnp.sum(route_weights, axis=1, keepdims=True)
    chosen = expert_ids[:, :, None] == jnp.arange(experts, dtype=jnp.int32)[None, None, :]
    combine = jnp.sum(jnp.where(chosen, shares[:, :, None], 0.0), axis=1)
    upper = combine.astype(BF16)
    lower = (combine - upper.astype(F32)).astype(BF16)
    extra = -(-2 * experts // 128) * 128
    pad = jnp.zeros((rows, extra - 2 * experts), BF16)
    packed = jnp.concatenate([normed, upper, lower, pad], axis=1)
    tokens = jnp.concatenate([swap(packed, s) for s in range(slots)], axis=0)

    total_rows = rows * slots
    tail = tokens[:, width:].astype(F32)
    upper_mine = lax.dynamic_slice_in_dim(tail, me * local_experts, local_experts, 1)
    lower_mine = lax.dynamic_slice_in_dim(tail, experts + me * local_experts, local_experts, 1)
    mine = upper_mine + lower_mine
    outs = [jnp.zeros((total_rows, part), F32) for _ in range(cores)]
    for e in range(local_experts):
        gate = sum(
            jnp.dot(tokens[:, j * part : (j + 1) * part], wg[j][e], preferred_element_type=F32)
            for j in range(cores)
        )
        up = sum(
            jnp.dot(tokens[:, j * part : (j + 1) * part], wu[j][e], preferred_element_type=F32)
            for j in range(cores)
        )
        active = (jax.nn.silu(gate) * up * mine[:, e : e + 1]).astype(BF16)
        outs = [
            o + jnp.dot(active, wd[j][e], preferred_element_type=F32) for j, o in enumerate(outs)
        ]
    produced = jnp.concatenate(outs, axis=1).astype(BF16)
    back = sum(
        swap(produced[s * rows : (s + 1) * rows], s).astype(F32) for s in range(slots)
    )
    result = mixed[:, :part] + back[:, :part]
    for m in range(1, cores):
        result = result + from_core(back[:, m * part : (m + 1) * part], m)
    return result.astype(BF16)


def solution(mesh):
    in_specs = (
        P(("groups", "dev", "pair"), None, None),
        P(("groups", "dev", "pair"), None, None, None),
        P(("groups", "dev", "pair"), None, None, None),
        P(("groups", "dev", "pair"), None, None),
        P(("groups", "dev", "pair"), None, None),
        P(("groups", "dev", "pair")),
        P("dev", "pair"),
        P(("groups", "dev"), "pair"),
        P("pair"),
        P(("groups", "dev"), None),
        P(("groups", "dev"), None),
        P("dev", "pair", None),
        P("dev", "pair", None),
        P("dev", None, "pair"),
    )
    out_specs = P(("groups", "dev"), "pair")
    return jax.shard_map(
        per_device, mesh=mesh, in_specs=in_specs, out_specs=out_specs, check_vma=False
    )
```

```python
import functools
import math

import jax
import jax.numpy as jnp
from jax import lax
from jax.experimental import pallas as pl
from jax.experimental.pallas import tpu as pltpu
from jax.sharding import PartitionSpec as P

F32 = jnp.float32
BF16 = jnp.bfloat16
VMEM = pl.BlockSpec(memory_space=pltpu.VMEM)
SMEM = pl.BlockSpec(memory_space=pltpu.SMEM)
ANY = pl.BlockSpec(memory_space=pl.ANY)
MIB = 1024 * 1024


def choose(core, values):
    result = jnp.int32(values[0])
    for c in range(1, len(values)):
        result = jnp.where(core == c, jnp.int32(values[c]), result)
    return result


def turned(value, m, cores):
    band = value.shape[0] // cores
    pieces = [value[i * band : (i + 1) * band] for i in range(cores)]
    return jnp.concatenate([pieces[i ^ m] for i in range(cores)], axis=0) if m else value


def from_natural(core, value, cores):
    result = value
    for c in range(1, cores):
        result = jnp.where(core == c, turned(value, c, cores), result)
    return result


def attend_kernel(
    kv_heads, offset, len_ref, place_ref, q_ref, k_hbm, v_hbm, ik_ref, iv_ref, *refs
):
    cores, slots = len(offset), len(offset[0])
    out_refs = refs[:cores]
    k_buf, v_buf, mask_ref, all_ref, sems = refs[cores:]
    rows, heads, size = q_ref.shape
    span = k_buf.shape[1]
    per = heads // kv_heads
    block = heads // (cores * slots)
    scale = size ** (-0.5) * math.log2(math.e)
    step = 2

    def copies(r):
        return (
            pltpu.make_async_copy(k_hbm.at[r], k_buf.at[r], sems.at[0, r]),
            pltpu.make_async_copy(v_hbm.at[r], v_buf.at[r], sems.at[1, r]),
        )

    for r in range(rows):
        for copy in copies(r):
            copy.start()
    column = lax.broadcasted_iota(jnp.int32, (heads, span), 1)
    head = lax.broadcasted_iota(jnp.int32, (heads, span), 0)
    mask_ref[...] = jnp.where(lax.rem(column, kv_heads) == head // per, column, 1 << 30)

    def spread(value):
        return jnp.concatenate(
            [
                jnp.broadcast_to(value[g : g + 1, :].astype(F32), (per, size))
                for g in range(kv_heads)
            ],
            axis=0,
        )

    def one(r):
        q = q_ref[r]
        scores = lax.dot_general(
            q, k_buf[r], (((1,), (1,)), ((), ())), preferred_element_type=F32
        )
        scores = jnp.where(mask_ref[...] < len_ref[r] * kv_heads, scores, -1e30)
        own = jnp.sum(q.astype(F32) * spread(ik_ref[r]), axis=1, keepdims=True)
        peak = jnp.maximum(jnp.max(scores, axis=1, keepdims=True), own)
        expo = jnp.exp2((scores - peak) * scale)
        fresh = jnp.exp2((own - peak) * scale)
        total = jnp.sum(expo, axis=1, keepdims=True) + fresh
        accum = jnp.dot(expo.astype(BF16), v_buf[r], preferred_element_type=F32)
        all_ref[pl.ds(r, heads, stride=rows), :] = (accum + fresh * spread(iv_ref[r])) / total

    def body(i, carry):
        for j in range(step):
            for copy in copies(i * step + j):
                copy.wait()
        for j in range(step):
            one(i * step + j)
        return carry

    lax.fori_loop(0, rows // step, body, 0)
    me, core = place_ref[0], place_ref[1]
    for m in range(cores):
        for s in range(slots):
            which = me ^ choose(core, [offset[c ^ m][s] for c in range(cores)])
            for h in range(block):
                at = pl.multiple_of((which * block + h) * rows, rows)
                out_refs[m][s, :, h * size : (h + 1) * size] = all_ref[
                    pl.ds(at, rows), :
                ].astype(BF16)


def attend(query, keys, values, fresh_key, fresh_value, lengths, place, offset):
    rows, heads, size = query.shape
    positions, kv_heads = keys.shape[1:3]
    span = positions * kv_heads
    cores, slots = len(offset), len(offset[0])
    width = heads * size // (cores * slots)
    return pl.pallas_call(
        functools.partial(attend_kernel, kv_heads, offset),
        out_shape=[jax.ShapeDtypeStruct((slots, rows, width), BF16)] * cores,
        in_specs=[SMEM, SMEM, VMEM, ANY, ANY, VMEM, VMEM],
        out_specs=[VMEM] * cores,
        scratch_shapes=[
            pltpu.VMEM((rows, span, size), BF16),
            pltpu.VMEM((rows, span, size), BF16),
            pltpu.VMEM((heads, span), jnp.int32),
            pltpu.VMEM((heads * rows, size), F32),
            pltpu.SemaphoreType.DMA((2, rows)),
        ],
        compiler_params=pltpu.CompilerParams(vmem_limit_bytes=60 * MIB),
    )(
        lengths,
        place,
        query,
        keys.reshape(rows, span, size),
        values.reshape(rows, span, size),
        fresh_key,
        fresh_value,
    )


def take_slots(offset, place_ref, own_ref, moved_refs):
    core = place_ref[1]
    result = []
    for s, ref in enumerate(moved_refs):
        block = ref[...]
        for c in range(len(offset)):
            if offset[c][s] == 0:
                block = jnp.where(core == c, own_ref[...], block)
        result.append(block)
    return jnp.concatenate(result, axis=0)


def project_kernel(offset, place_ref, own_ref, *refs):
    cores, slots = len(offset), len(offset[0])
    moved_refs, w_refs = refs[:slots], refs[slots : slots + cores]
    out_refs = refs[slots + cores : 2 * slots + cores]
    left = take_slots(offset, place_ref, own_ref, moved_refs)
    rows, part = own_ref.shape[0], w_refs[0].shape[1]
    for j in range(cores):
        product = jnp.dot(left, w_refs[j][...], preferred_element_type=F32).astype(BF16)
        for s in range(slots):
            out_refs[s][:, j * part : (j + 1) * part] = product[s * rows : (s + 1) * rows]


def project(place, own, moved, weights, offset):
    rows = own.shape[0]
    depth, part = weights[0].shape
    cores, slots = len(offset), len(offset[0])
    return pl.pallas_call(
        functools.partial(project_kernel, offset),
        out_shape=[jax.ShapeDtypeStruct((rows, part * cores), BF16)] * slots,
        in_specs=[SMEM, VMEM] + [VMEM] * (slots + cores),
        out_specs=[VMEM] * slots,
        compiler_params=pltpu.CompilerParams(vmem_limit_bytes=12 * MIB),
    )(place, own, *moved, *weights)


def norm_kernel(cores, experts, place_ref, *refs):
    sums_refs, stream_refs, gain_refs = refs[:cores], refs[cores : 2 * cores], refs[2 * cores : 3 * cores]
    ids_ref, routes_ref, mixed_ref, out_ref = refs[3 * cores :]
    rows, part = stream_refs[0].shape
    width = part * cores
    core = place_ref[1]
    squares = 0.0
    mixed = []
    for j in range(cores):
        block = from_natural(core, stream_refs[j][...].astype(F32), cores)
        for m in range(cores):
            other = sums_refs[m][:, (j ^ m) * part : ((j ^ m) + 1) * part]
            block = block + turned(other, m, cores)
        mixed.append(block)
        squares = squares + jnp.sum(block * block, axis=1, keepdims=True)
    mixed_ref[...] = mixed[0]
    scale = lax.rsqrt(squares / width + 1e-06)
    for j in range(cores):
        out_ref[:, j * part : (j + 1) * part] = (mixed[j] * scale * gain_refs[j][...]).astype(BF16)
    picks = ids_ref.shape[0]
    extra = out_ref.shape[1] - width
    ids, routes = ids_ref[...], routes_ref[...]
    shares = routes / jnp.sum(routes, axis=0, keepdims=True)
    line = lax.broadcasted_iota(jnp.int32, (extra, rows), 0)
    line = jnp.where(line < experts, line, line - experts)
    combine = jnp.zeros((extra, rows), F32)
    for k in range(picks):
        combine = jnp.where(ids[k : k + 1, :] == line, shares[k : k + 1, :], combine)
    combine = jnp.concatenate([combine, jnp.zeros((extra, 128 - rows), F32)], axis=1)
    combine = from_natural(core, jnp.transpose(combine)[:rows], cores)
    upper = combine.astype(BF16)
    lower = (combine - upper.astype(F32)).astype(BF16)
    lane = lax.broadcasted_iota(jnp.int32, (rows, extra), 1)
    out_ref[:, width:] = jnp.where(lane < experts, upper.astype(F32), lower.astype(F32)).astype(BF16)


def normalise(place, sums, stream, gain, ids, routes, experts):
    rows, part = stream[0].shape
    cores = len(sums)
    extra = -(-2 * experts // 128) * 128
    return pl.pallas_call(
        functools.partial(norm_kernel, cores, experts),
        out_shape=(
            jax.ShapeDtypeStruct((rows, part), F32),
            jax.ShapeDtypeStruct((rows, part * cores + extra), BF16),
        ),
        in_specs=[SMEM] + [VMEM] * (3 * cores + 2),
        out_specs=(VMEM, VMEM),
        compiler_params=pltpu.CompilerParams(vmem_limit_bytes=8 * MIB),
    )(place, *sums, *stream, *gain, ids.T, routes.T)


def expert_kernel(offset, devs, place_ref, own_ref, *refs):
    cores, slots = len(offset), len(offset[0])
    moved_refs, refs = refs[:slots], refs[slots:]
    gate_refs, up_refs, down_refs = refs[:cores], refs[cores : 2 * cores], refs[2 * cores : 3 * cores]
    out_refs = refs[3 * cores : 3 * cores + slots]
    gate_buf, up_buf, down_buf, sems = refs[3 * cores + slots :]
    local, part, hidden = gate_refs[0].shape
    rows = own_ref.shape[0]
    width = part * cores

    def copy(kind, j, e):
        source = (gate_refs, up_refs, down_refs)[kind][j]
        target = (gate_buf, up_buf, down_buf)[kind]
        return pltpu.make_async_copy(source.at[e], target.at[j, e], sems.at[kind, j, e])

    for e in range(local):
        for kind in range(3):
            for j in range(cores):
                copy(kind, j, e).start()
    tokens = take_slots(offset, place_ref, own_ref, moved_refs)
    tail = tokens[:, width:].astype(F32)
    lane = lax.broadcasted_iota(jnp.int32, tail.shape, 1)
    experts = local * devs
    total = [0.0] * cores
    for e in range(local):
        mine = place_ref[0] * local + e
        share = jnp.sum(
            jnp.where((lane == mine) | (lane == mine + experts), tail, 0.0), axis=1, keepdims=True
        )
        sums = []
        for kind in range(2):
            value = 0.0
            for j in range(cores):
                copy(kind, j, e).wait()
                value = value + jnp.dot(
                    tokens[:, j * part : (j + 1) * part],
                    (gate_buf, up_buf)[kind][j, e],
                    preferred_element_type=F32,
                )
            sums.append(value)
        gate, up = sums
        active = (gate / (1.0 + jnp.exp(-gate)) * up * share).astype(BF16)
        for j in range(cores):
            copy(2, j, e).wait()
            total[j] = total[j] + jnp.dot(active, down_buf[j, e], preferred_element_type=F32)
    for j in range(cores):
        for s in range(slots):
            out_refs[s][:, j * part : (j + 1) * part] = total[j][
                s * rows : (s + 1) * rows
            ].astype(BF16)


def apply_experts(place, own, moved, gate, up, down, offset, devs):
    cores, slots = len(offset), len(offset[0])
    local, part, hidden = gate[0].shape
    rows = own.shape[0]
    return pl.pallas_call(
        functools.partial(expert_kernel, offset, devs),
        out_shape=[jax.ShapeDtypeStruct((rows, part * cores), BF16)] * slots,
        in_specs=[SMEM, VMEM] + [VMEM] * slots + [ANY] * (3 * cores),
        out_specs=[VMEM] * slots,
        scratch_shapes=[
            pltpu.VMEM((cores, local, part, hidden), BF16),
            pltpu.VMEM((cores, local, part, hidden), BF16),
            pltpu.VMEM((cores, local, hidden, part), BF16),
            pltpu.SemaphoreType.DMA((3, cores, local)),
        ],
        compiler_params=pltpu.CompilerParams(vmem_limit_bytes=56 * MIB),
    )(place, own, *moved, *gate, *up, *down)


def per_device(
    query,
    stored_keys,
    stored_values,
    incoming_key,
    incoming_value,
    lengths,
    out_weight,
    residual,
    norm_gain,
    expert_ids,
    route_weights,
    w_gate,
    w_up,
    w_down,
):
    devs = lax.axis_size("dev")
    cores = lax.axis_size("pair")
    me = lax.axis_index("dev")
    core = lax.axis_index("pair")
    slots = devs // cores
    offset = [[c * slots + s for s in range(slots)] for c in range(cores)]
    place = jnp.stack([me, core]).astype(jnp.int32)
    rows, part = residual.shape
    barrier = lax.optimization_barrier

    def from_core(value, m):
        return lax.ppermute(value, "pair", [(c, c ^ m) for c in range(cores)])

    def gathered(value):
        return [value] + [from_core(value, m) for m in range(1, cores)]

    def swap(value, s):
        pairs = [
            (d * cores + c, (d ^ offset[c][s]) * cores + c)
            for d in range(devs)
            for c in range(cores)
            if offset[c][s]
        ]
        return lax.ppermute(value, ("dev", "pair"), pairs)

    own_slot = [[c for c in range(cores) if offset[c][s] == 0] for s in range(slots)]

    def total_of(own, moved):
        result = 0.0
        for s in range(slots):
            block = moved[s]
            for c in own_slot[s]:
                block = jnp.where(core == c, own[s], block)
            result = result + block.astype(F32)
        return result

    def own_block(blocks):
        return blocks[[s for s in range(slots) if own_slot[s]][0]]

    stream = gathered(residual)
    gain = gathered(norm_gain.reshape(1, part))
    wg = gathered(w_gate)
    wu = gathered(w_up)
    attended = attend(
        query, stored_keys, stored_values, incoming_key, incoming_value, lengths, place, offset
    )
    attended, wg, wu, stream, gain = barrier((attended, wg, wu, stream, gain))
    held = [attended[0]] + [from_core(attended[m], m) for m in range(1, cores)]
    held, out_weight, w_down = barrier((held, out_weight, w_down))
    wo = gathered(out_weight)
    outgoing = [jnp.concatenate([h[s] for h in held], axis=0) for s in range(slots)]
    arrived = [swap(outgoing[s], s) for s in range(slots)]
    arrived, wo, w_down = barrier((arrived, wo, w_down))
    wd = gathered(w_down)
    partial = project(place, own_block(outgoing), arrived, wo, offset)
    sums = total_of(partial, [swap(partial[s], s) for s in range(slots)])
    sums, wd = barrier((sums, wd))
    mixed, packed = normalise(
        place, gathered(sums), stream, gain, expert_ids, route_weights, w_gate.shape[0] * devs
    )
    tokens = [swap(packed, s) for s in range(slots)]
    produced = apply_experts(place, packed, tokens, wg, wu, wd, offset, devs)
    back = total_of(produced, [swap(produced[s], s) for s in range(slots)])
    result = mixed + back[:, :part]
    for m in range(1, cores):
        other = from_core(back[:, m * part : (m + 1) * part], m)
        result = result + turned(other, m, cores)
    return from_natural(core, result, cores).astype(BF16)


def solution(mesh):
    in_specs = (
        P(("groups", "dev", "pair"), None, None),
        P(("groups", "dev", "pair"), None, None, None),
        P(("groups", "dev", "pair"), None, None, None),
        P(("groups", "dev", "pair"), None, None),
        P(("groups", "dev", "pair"), None, None),
        P(("groups", "dev", "pair")),
        P("dev", "pair"),
        P(("groups", "dev"), "pair"),
        P("pair"),
        P(("groups", "dev"), None),
        P(("groups", "dev"), None),
        P("dev", "pair", None),
        P("dev", "pair", None),
        P("dev", None, "pair"),
    )
    out_specs = P(("groups", "dev"), "pair")
    return jax.shard_map(
        per_device, mesh=mesh, in_specs=in_specs, out_specs=out_specs, check_vma=False
    )
```

```python
import functools
import math

import jax
import jax.numpy as jnp
from jax import lax
from jax.experimental import pallas as pl
from jax.experimental.pallas import tpu as pltpu
from jax.sharding import PartitionSpec as P

F32 = jnp.float32
BF16 = jnp.bfloat16
VMEM = pl.BlockSpec(memory_space=pltpu.VMEM)
SMEM = pl.BlockSpec(memory_space=pltpu.SMEM)
ANY = pl.BlockSpec(memory_space=pl.ANY)
MIB = 1024 * 1024
TUNED = {(8, 2): ((5, 0, 3, 6), (7, 1, 2, 4))}


def choose(core, values):
    result = jnp.int32(values[0])
    for c in range(1, len(values)):
        result = jnp.where(core == c, jnp.int32(values[c]), result)
    return result


def turned(value, m, cores):
    band = value.shape[0] // cores
    pieces = [value[i * band : (i + 1) * band] for i in range(cores)]
    return jnp.concatenate([pieces[i ^ m] for i in range(cores)], axis=0) if m else value


def from_natural(core, value, cores):
    result = value
    for c in range(1, cores):
        result = jnp.where(core == c, turned(value, c, cores), result)
    return result


def attend_kernel(
    kv_heads, offset, len_ref, me_ref, core_ref, q_ref, k_hbm, v_hbm, ik_ref, iv_ref, *refs
):
    cores, slots = len(offset), len(offset[0])
    out_refs = refs[:cores]
    k_buf, v_buf, mask_ref, all_ref, order_ref, sems = refs[cores:]
    rows, heads, size = q_ref.shape
    span = k_buf.shape[1]
    per = heads // kv_heads
    block = heads // (cores * slots)
    scale = size ** (-0.5) * math.log2(math.e)
    step = 4
    chunks = 4
    chunk = span // chunks

    lengths = [len_ref[r] for r in range(rows)]
    ranks = [jnp.int32(0)] * rows
    for i in range(rows):
        for j in range(i + 1, rows):
            later = (lengths[i] < lengths[j]).astype(jnp.int32)
            ranks[i] = ranks[i] + later
            ranks[j] = ranks[j] + (1 - later)
    for r in range(rows):
        order_ref[ranks[r]] = jnp.int32(r)

    def copies(i, used):
        r = order_ref[i]
        part = pl.ds(0, used)
        return (
            pltpu.make_async_copy(k_hbm.at[r, part], k_buf.at[r, part], sems.at[0, i]),
            pltpu.make_async_copy(v_hbm.at[r, part], v_buf.at[r, part], sems.at[1, i]),
        )

    def by_length(i, work):
        needed = (len_ref[order_ref[i * step]] * kv_heads + (chunk - 1)) // chunk
        for n in range(1, chunks + 1):

            @pl.when(needed == n)
            def _():
                work(n * chunk)

    def begin(i, carry):
        def work(used):
            for j in range(step):
                for copy in copies(i * step + j, used):
                    copy.start()

        by_length(i, work)
        return carry

    lax.fori_loop(0, rows // step, begin, 0)
    column = lax.broadcasted_iota(jnp.int32, (heads, span), 1)
    head = lax.broadcasted_iota(jnp.int32, (heads, span), 0)
    mask_ref[...] = jnp.where((column & (kv_heads - 1)) == (head >> (per.bit_length() - 1)), column, 1 << 30)

    def spread(value):
        return jnp.concatenate(
            [
                jnp.broadcast_to(value[g : g + 1, :].astype(F32), (per, size))
                for g in range(kv_heads)
            ],
            axis=0,
        )

    def several(group, used):
        queries = [q_ref[r] for r in group]
        scores = [
            lax.dot_general(
                q, k_buf[r, :used], (((1,), (1,)), ((), ())), preferred_element_type=F32
            )
            for q, r in zip(queries, group)
        ]
        own = [
            jnp.sum(q.astype(F32) * spread(ik_ref[r]), axis=1, keepdims=True)
            for q, r in zip(queries, group)
        ]
        scores = [
            jnp.where(mask_ref[:, :used] < len_ref[r] * kv_heads, x, -1e30)
            for x, r in zip(scores, group)
        ]
        peak = [
            jnp.maximum(jnp.max(x, axis=1, keepdims=True), o) for x, o in zip(scores, own)
        ]
        expo = [jnp.exp2((x - p) * scale) for x, p in zip(scores, peak)]
        accum = [
            jnp.dot(x.astype(BF16), v_buf[r, :used], preferred_element_type=F32)
            for x, r in zip(expo, group)
        ]
        fresh = [jnp.exp2((o - p) * scale) for o, p in zip(own, peak)]
        total = [jnp.sum(x, axis=1, keepdims=True) + f for x, f in zip(expo, fresh)]
        for x, f, t, r in zip(accum, fresh, total, group):
            all_ref[pl.ds(r, heads, stride=rows), :] = (x + f * spread(iv_ref[r])) / t

    def body(i, carry):
        def work(used):
            for j in range(step):
                for copy in copies(i * step + j, used):
                    copy.wait()
            several([order_ref[i * step + j] for j in range(step)], used)

        by_length(i, work)
        return carry

    lax.fori_loop(0, rows // step, body, 0)
    me, core = me_ref[0], core_ref[0]
    for m in range(cores):
        for s in range(slots):
            which = me ^ choose(core, [offset[c ^ m][s] for c in range(cores)])
            for h in range(block):
                at = pl.multiple_of((which * block + h) * rows, rows)
                out_refs[m][s, :, h * size : (h + 1) * size] = all_ref[
                    pl.ds(at, rows), :
                ].astype(BF16)


def attend(query, keys, values, fresh_key, fresh_value, lengths, place, offset):
    rows, heads, size = query.shape
    positions, kv_heads = keys.shape[1:3]
    span = positions * kv_heads
    cores, slots = len(offset), len(offset[0])
    width = heads * size // (cores * slots)
    return pl.pallas_call(
        functools.partial(attend_kernel, kv_heads, offset),
        out_shape=[jax.ShapeDtypeStruct((slots, rows, width), BF16)] * cores,
        in_specs=[SMEM, SMEM, SMEM, VMEM, ANY, ANY, VMEM, VMEM],
        out_specs=[VMEM] * cores,
        scratch_shapes=[
            pltpu.VMEM((rows, span, size), BF16),
            pltpu.VMEM((rows, span, size), BF16),
            pltpu.VMEM((heads, span), jnp.int32),
            pltpu.VMEM((heads * rows, size), F32),
            pltpu.SMEM((rows,), jnp.int32),
            pltpu.SemaphoreType.DMA((2, rows)),
        ],
        compiler_params=pltpu.CompilerParams(vmem_limit_bytes=60 * MIB),
    )(
        lengths,
        *place,
        query,
        keys.reshape(rows, span, size),
        values.reshape(rows, span, size),
        fresh_key,
        fresh_value,
    )


def take_slots(offset, core_ref, own_ref, moved_refs):
    core = core_ref[0]
    result = []
    for s, ref in enumerate(moved_refs):
        block = ref[...]
        for c in range(len(offset)):
            if offset[c][s] == 0:
                block = jnp.where(core == c, own_ref[...], block)
        result.append(block)
    return jnp.concatenate(result, axis=0)


def project_kernel(offset, core_ref, own_ref, *refs):
    cores, slots = len(offset), len(offset[0])
    moved_refs, w_refs = refs[:slots], refs[slots : slots + cores]
    out_refs = refs[slots + cores : 2 * slots + cores]
    left = take_slots(offset, core_ref, own_ref, moved_refs)
    rows, part = own_ref.shape[0], w_refs[0].shape[1]
    for j in range(cores):
        product = jnp.dot(left, w_refs[j][...], preferred_element_type=F32).astype(BF16)
        for s in range(slots):
            out_refs[s][:, j * part : (j + 1) * part] = product[s * rows : (s + 1) * rows]


def project(place, own, moved, weights, offset):
    rows = own.shape[0]
    depth, part = weights[0].shape
    cores, slots = len(offset), len(offset[0])
    return pl.pallas_call(
        functools.partial(project_kernel, offset),
        out_shape=[jax.ShapeDtypeStruct((rows, part * cores), BF16)] * slots,
        in_specs=[SMEM, VMEM] + [VMEM] * (slots + cores),
        out_specs=[VMEM] * slots,
        compiler_params=pltpu.CompilerParams(vmem_limit_bytes=12 * MIB),
    )(place[1], own, *moved, *weights)


def norm_kernel(cores, experts, core_ref, *refs):
    sums_refs, stream_refs, gain_refs = refs[:cores], refs[cores : 2 * cores], refs[2 * cores : 3 * cores]
    ids_ref, routes_ref, mixed_ref, out_ref = refs[3 * cores :]
    rows, part = stream_refs[0].shape
    width = part * cores
    core = core_ref[0]
    squares = 0.0
    mixed = []
    for j in range(cores):
        block = from_natural(core, stream_refs[j][...].astype(F32), cores)
        for m in range(cores):
            other = sums_refs[m][:, (j ^ m) * part : ((j ^ m) + 1) * part]
            block = block + turned(other, m, cores)
        mixed.append(block)
        squares = squares + jnp.sum(block * block, axis=1, keepdims=True)
    mixed_ref[...] = mixed[0]
    scale = lax.rsqrt(squares / width + 1e-06)
    for j in range(cores):
        out_ref[:, j * part : (j + 1) * part] = (mixed[j] * scale * gain_refs[j][...]).astype(BF16)
    picks = ids_ref.shape[0]
    extra = out_ref.shape[1] - width
    ids, routes = ids_ref[...], routes_ref[...]
    shares = routes / jnp.sum(routes, axis=0, keepdims=True)
    line = lax.broadcasted_iota(jnp.int32, (extra, rows), 0)
    line = jnp.where(line < experts, line, line - experts)
    combine = jnp.zeros((extra, rows), F32)
    for k in range(picks):
        combine = jnp.where(ids[k : k + 1, :] == line, shares[k : k + 1, :], combine)
    combine = jnp.concatenate([combine, jnp.zeros((extra, 128 - rows), F32)], axis=1)
    combine = from_natural(core, jnp.transpose(combine)[:rows], cores)
    upper = combine.astype(BF16)
    lower = (combine - upper.astype(F32)).astype(BF16)
    lane = lax.broadcasted_iota(jnp.int32, (rows, extra), 1)
    out_ref[:, width:] = jnp.where(lane < experts, upper.astype(F32), lower.astype(F32)).astype(BF16)


def normalise(place, sums, stream, gain, ids, routes, experts):
    rows, part = stream[0].shape
    cores = len(sums)
    extra = -(-2 * experts // 128) * 128
    return pl.pallas_call(
        functools.partial(norm_kernel, cores, experts),
        out_shape=(
            jax.ShapeDtypeStruct((rows, part), F32),
            jax.ShapeDtypeStruct((rows, part * cores + extra), BF16),
        ),
        in_specs=[SMEM] + [VMEM] * (3 * cores + 2),
        out_specs=(VMEM, VMEM),
        compiler_params=pltpu.CompilerParams(vmem_limit_bytes=8 * MIB),
    )(place[1], *sums, *stream, *gain, ids.T, routes.T)


def fetch_kernel(count, *refs):
    sources, targets, sems = refs[:count], refs[count : 2 * count], refs[2 * count]
    copies = [
        pltpu.make_async_copy(sources[i].at[0], targets[i], sems.at[i]) for i in range(count)
    ]
    for copy in copies:
        copy.start()
    for copy in copies:
        copy.wait()


def fetch(weights):
    count = len(weights)
    return pl.pallas_call(
        functools.partial(fetch_kernel, count),
        out_shape=[jax.ShapeDtypeStruct(w.shape[1:], w.dtype) for w in weights],
        in_specs=[ANY] * count,
        out_specs=[VMEM] * count,
        scratch_shapes=[pltpu.SemaphoreType.DMA((count,))],
        compiler_params=pltpu.CompilerParams(vmem_limit_bytes=43 * MIB),
    )(*weights)


def expert_kernel(offset, devs, me_ref, core_ref, own_ref, *refs):
    cores, slots = len(offset), len(offset[0])
    moved_refs, refs = refs[:slots], refs[slots:]
    first_refs, refs = refs[: 3 * cores], refs[3 * cores :]
    weight_refs = refs[: 3 * cores]
    out_refs = refs[3 * cores : 3 * cores + slots]
    gate_buf, up_buf, down_buf, sems = refs[3 * cores + slots :]
    local, part, hidden = weight_refs[0].shape
    rows = own_ref.shape[0]
    width = part * cores
    bufs = (gate_buf, up_buf, down_buf)

    def copy(kind, j, e):
        return pltpu.make_async_copy(
            weight_refs[kind * cores + j].at[e], bufs[kind].at[j, e - 1], sems.at[kind, j, e - 1]
        )

    def weight(kind, j, e):
        if e == 0:
            return first_refs[kind * cores + j][...]
        copy(kind, j, e).wait()
        return bufs[kind][j, e - 1]

    for e in range(1, local):
        for kind in range(3):
            for j in range(cores):
                copy(kind, j, e).start()
    tokens = take_slots(offset, core_ref, own_ref, moved_refs)
    tail = tokens[:, width:].astype(F32)
    lane = lax.broadcasted_iota(jnp.int32, tail.shape, 1)
    experts = local * devs
    total = [0.0] * cores
    for e in range(local):
        mine = me_ref[0] * local + e
        share = jnp.sum(
            jnp.where((lane == mine) | (lane == mine + experts), tail, 0.0), axis=1, keepdims=True
        )
        sums = []
        for kind in range(2):
            value = 0.0
            for j in range(cores):
                value = value + jnp.dot(
                    tokens[:, j * part : (j + 1) * part],
                    weight(kind, j, e),
                    preferred_element_type=F32,
                )
            sums.append(value)
        gate, up = sums
        active = (gate / (1.0 + jnp.exp(-gate)) * up * share).astype(BF16)
        for j in range(cores):
            total[j] = total[j] + jnp.dot(active, weight(2, j, e), preferred_element_type=F32)
    for j in range(cores):
        for s in range(slots):
            out_refs[s][:, j * part : (j + 1) * part] = total[j][
                s * rows : (s + 1) * rows
            ].astype(BF16)


def apply_experts(place, own, moved, first, weights, offset, devs):
    cores, slots = len(offset), len(offset[0])
    local, part, hidden = weights[0].shape
    rows = own.shape[0]
    return pl.pallas_call(
        functools.partial(expert_kernel, offset, devs),
        out_shape=[jax.ShapeDtypeStruct((rows, part * cores), BF16)] * slots,
        in_specs=[SMEM, SMEM, VMEM] + [VMEM] * (slots + 3 * cores) + [ANY] * (3 * cores),
        out_specs=[VMEM] * slots,
        scratch_shapes=[
            pltpu.VMEM((cores, local - 1, part, hidden), BF16),
            pltpu.VMEM((cores, local - 1, part, hidden), BF16),
            pltpu.VMEM((cores, local - 1, hidden, part), BF16),
            pltpu.SemaphoreType.DMA((3, cores, local - 1)),
        ],
        compiler_params=pltpu.CompilerParams(vmem_limit_bytes=43 * MIB),
    )(*place, own, *moved, *first, *weights)


def per_device(
    query,
    stored_keys,
    stored_values,
    incoming_key,
    incoming_value,
    lengths,
    out_weight,
    residual,
    norm_gain,
    expert_ids,
    route_weights,
    w_gate,
    w_up,
    w_down,
):
    devs = lax.axis_size("dev")
    cores = lax.axis_size("pair")
    me = lax.axis_index("dev")
    core = lax.axis_index("pair")
    slots = devs // cores
    offset = TUNED.get(
        (devs, cores), [[c * slots + s for s in range(slots)] for c in range(cores)]
    )
    place = (me.astype(jnp.int32).reshape(1), core.astype(jnp.int32).reshape(1))
    rows, part = residual.shape
    barrier = lax.optimization_barrier

    def from_core(value, m):
        return lax.ppermute(value, "pair", [(c, c ^ m) for c in range(cores)])

    def gathered(value):
        return [value] + [from_core(value, m) for m in range(1, cores)]

    def swap(value, s):
        pairs = [
            (d * cores + c, (d ^ offset[c][s]) * cores + c)
            for d in range(devs)
            for c in range(cores)
            if offset[c][s]
        ]
        return lax.ppermute(value, ("dev", "pair"), pairs)

    own_slot = [[c for c in range(cores) if offset[c][s] == 0] for s in range(slots)]

    def total_of(own, moved):
        result = 0.0
        for s in range(slots):
            block = moved[s]
            for c in own_slot[s]:
                block = jnp.where(core == c, own[s], block)
            result = result + block.astype(F32)
        return result

    def own_block(blocks):
        return blocks[[s for s in range(slots) if own_slot[s]][0]]

    stream = gathered(residual)
    gain = gathered(norm_gain.reshape(1, part))
    wg = gathered(w_gate)
    attended = attend(
        query, stored_keys, stored_values, incoming_key, incoming_value, lengths, place, offset
    )
    attended, wg, stream, gain = barrier((attended, wg, stream, gain))
    held = [attended[0]] + [from_core(attended[m], m) for m in range(1, cores)]
    held, out_weight, w_up, w_down = barrier((held, out_weight, w_up, w_down))
    wo = gathered(out_weight)
    outgoing = [jnp.concatenate([h[s] for h in held], axis=0) for s in range(slots)]
    arrived = [swap(outgoing[s], s) for s in range(slots)]
    arrived, wo, w_up, w_down = barrier((arrived, wo, w_up, w_down))
    wu = gathered(w_up)
    partial = project(place, own_block(outgoing), arrived, wo, offset)
    sums = total_of(partial, [swap(partial[s], s) for s in range(slots)])
    sums, wu, w_down = barrier((sums, wu, w_down))
    mixed, packed = normalise(
        place, gathered(sums), stream, gain, expert_ids, route_weights, w_gate.shape[0] * devs
    )
    packed, weights, w_down = barrier((packed, wg + wu, w_down))
    tokens = [swap(packed, s) for s in range(slots)]
    weights = weights + gathered(w_down)
    first = fetch(weights)
    produced = apply_experts(place, packed, tokens, first, weights, offset, devs)
    back = total_of(produced, [swap(produced[s], s) for s in range(slots)])
    result = mixed + back[:, :part]
    for m in range(1, cores):
        other = from_core(back[:, m * part : (m + 1) * part], m)
        result = result + turned(other, m, cores)
    return from_natural(core, result, cores).astype(BF16)


def solution(mesh):
    in_specs = (
        P(("groups", "dev", "pair"), None, None),
        P(("groups", "dev", "pair"), None, None, None),
        P(("groups", "dev", "pair"), None, None, None),
        P(("groups", "dev", "pair"), None, None),
        P(("groups", "dev", "pair"), None, None),
        P(("groups", "dev", "pair")),
        P("dev", "pair"),
        P(("groups", "dev"), "pair"),
        P("pair"),
        P(("groups", "dev"), None),
        P(("groups", "dev"), None),
        P("dev", "pair", None),
        P("dev", "pair", None),
        P("dev", None, "pair"),
    )
    out_specs = P(("groups", "dev"), "pair")
    return jax.shard_map(
        per_device, mesh=mesh, in_specs=in_specs, out_specs=out_specs, check_vma=False
    )
```

```python
import functools
import math

import jax
import jax.numpy as jnp
from jax import lax
from jax.experimental import pallas as pl
from jax.experimental.pallas import tpu as pltpu
from jax.sharding import PartitionSpec as P

F32 = jnp.float32
BF16 = jnp.bfloat16
VMEM = pl.BlockSpec(memory_space=pltpu.VMEM)
SMEM = pl.BlockSpec(memory_space=pltpu.SMEM)
ANY = pl.BlockSpec(memory_space=pl.ANY)
MIB = 1024 * 1024
TUNED = {(8, 2): ((5, 0, 3, 6), (7, 1, 2, 4))}


def choose(core, values):
    result = jnp.int32(values[0])
    for c in range(1, len(values)):
        result = jnp.where(core == c, jnp.int32(values[c]), result)
    return result


def turned(value, m, cores):
    band = value.shape[0] // cores
    pieces = [value[i * band : (i + 1) * band] for i in range(cores)]
    return jnp.concatenate([pieces[i ^ m] for i in range(cores)], axis=0) if m else value


def from_natural(core, value, cores):
    result = value
    for c in range(1, cores):
        result = jnp.where(core == c, turned(value, c, cores), result)
    return result


def attend_kernel(
    kv_heads, offset, len_ref, me_ref, core_ref, q_hbm, k_hbm, v_hbm, ik_hbm, iv_hbm, *refs
):
    cores, slots = len(offset), len(offset[0])
    out_refs = refs[:cores]
    q_ref, ik_ref, iv_ref, k_buf, v_buf, mask_ref, all_ref, order_ref, sems, small_sems = refs[cores:]
    rows, heads, size = q_ref.shape
    span = k_buf.shape[1]
    per = heads // kv_heads
    block = heads // (cores * slots)
    scale = size ** (-0.5) * math.log2(math.e)
    step = 4
    chunks = 4
    chunk = span // chunks

    small = [
        pltpu.make_async_copy(source, target, small_sems.at[n])
        for n, (source, target) in enumerate(
            ((q_hbm, q_ref), (ik_hbm, ik_ref), (iv_hbm, iv_ref))
        )
    ]
    for copy in small:
        copy.start()

    lengths = [len_ref[r] for r in range(rows)]
    ranks = [jnp.int32(0)] * rows
    for i in range(rows):
        for j in range(i + 1, rows):
            later = (lengths[i] < lengths[j]).astype(jnp.int32)
            ranks[i] = ranks[i] + later
            ranks[j] = ranks[j] + (1 - later)
    for r in range(rows):
        order_ref[ranks[r]] = jnp.int32(r)

    def copies(i, used):
        r = order_ref[i]
        part = pl.ds(0, used)
        return (
            pltpu.make_async_copy(k_hbm.at[r, part], k_buf.at[r, part], sems.at[0, i]),
            pltpu.make_async_copy(v_hbm.at[r, part], v_buf.at[r, part], sems.at[1, i]),
        )

    def by_length(i, work):
        needed = (len_ref[order_ref[i * step]] * kv_heads + (chunk - 1)) // chunk
        for n in range(1, chunks + 1):

            @pl.when(needed == n)
            def _():
                work(n * chunk)

    def begin(i, carry):
        def work(used):
            for j in range(step):
                for copy in copies(i * step + j, used):
                    copy.start()

        by_length(i, work)
        return carry

    lax.fori_loop(0, rows // step, begin, 0)
    column = lax.broadcasted_iota(jnp.int32, (heads, span), 1)
    head = lax.broadcasted_iota(jnp.int32, (heads, span), 0)
    mask_ref[...] = jnp.where((column & (kv_heads - 1)) == (head >> (per.bit_length() - 1)), column, 1 << 30)

    def spread(value):
        return jnp.concatenate(
            [
                jnp.broadcast_to(value[g : g + 1, :].astype(F32), (per, size))
                for g in range(kv_heads)
            ],
            axis=0,
        )

    def several(group, used):
        queries = [q_ref[r] for r in group]
        scores = [
            lax.dot_general(
                q, k_buf[r, :used], (((1,), (1,)), ((), ())), preferred_element_type=F32
            )
            for q, r in zip(queries, group)
        ]
        own = [
            jnp.sum(q.astype(F32) * spread(ik_ref[r]), axis=1, keepdims=True)
            for q, r in zip(queries, group)
        ]
        scores = [
            jnp.where(mask_ref[:, :used] < len_ref[r] * kv_heads, x, -1e30)
            for x, r in zip(scores, group)
        ]
        peak = [
            jnp.maximum(jnp.max(x, axis=1, keepdims=True), o) for x, o in zip(scores, own)
        ]
        expo = [jnp.exp2((x - p) * scale) for x, p in zip(scores, peak)]
        accum = [
            jnp.dot(x.astype(BF16), v_buf[r, :used], preferred_element_type=F32)
            for x, r in zip(expo, group)
        ]
        fresh = [jnp.exp2((o - p) * scale) for o, p in zip(own, peak)]
        total = [jnp.sum(x, axis=1, keepdims=True) + f for x, f in zip(expo, fresh)]
        for x, f, t, r in zip(accum, fresh, total, group):
            all_ref[pl.ds(r, heads, stride=rows), :] = (x + f * spread(iv_ref[r])) / t

    def body(i, carry):
        def work(used):
            for j in range(step):
                for copy in copies(i * step + j, used):
                    copy.wait()
            several([order_ref[i * step + j] for j in range(step)], used)

        by_length(i, work)
        return carry

    for copy in small:
        copy.wait()
    lax.fori_loop(0, rows // step, body, 0)
    me, core = me_ref[0], core_ref[0]
    for m in range(cores):
        for s in range(slots):
            which = me ^ choose(core, [offset[c ^ m][s] for c in range(cores)])
            for h in range(block):
                at = pl.multiple_of((which * block + h) * rows, rows)
                out_refs[m][s, :, h * size : (h + 1) * size] = all_ref[
                    pl.ds(at, rows), :
                ].astype(BF16)


def attend(query, keys, values, fresh_key, fresh_value, lengths, place, offset):
    rows, heads, size = query.shape
    positions, kv_heads = keys.shape[1:3]
    span = positions * kv_heads
    cores, slots = len(offset), len(offset[0])
    width = heads * size // (cores * slots)
    return pl.pallas_call(
        functools.partial(attend_kernel, kv_heads, offset),
        out_shape=[jax.ShapeDtypeStruct((slots, rows, width), BF16)] * cores,
        in_specs=[SMEM, SMEM, SMEM] + [ANY] * 5,
        out_specs=[VMEM] * cores,
        scratch_shapes=[
            pltpu.VMEM(query.shape, BF16),
            pltpu.VMEM(fresh_key.shape, BF16),
            pltpu.VMEM(fresh_value.shape, BF16),
            pltpu.VMEM((rows, span, size), BF16),
            pltpu.VMEM((rows, span, size), BF16),
            pltpu.VMEM((heads, span), jnp.int32),
            pltpu.VMEM((heads * rows, size), F32),
            pltpu.SMEM((rows,), jnp.int32),
            pltpu.SemaphoreType.DMA((2, rows)),
            pltpu.SemaphoreType.DMA((3,)),
        ],
        compiler_params=pltpu.CompilerParams(vmem_limit_bytes=60 * MIB),
    )(
        lengths,
        *place,
        query,
        keys.reshape(rows, span, size),
        values.reshape(rows, span, size),
        fresh_key,
        fresh_value,
    )


def take_slots(offset, core_ref, own_ref, moved_refs):
    core = core_ref[0]
    result = []
    for s, ref in enumerate(moved_refs):
        block = ref[...]
        for c in range(len(offset)):
            if offset[c][s] == 0:
                block = jnp.where(core == c, own_ref[...], block)
        result.append(block)
    return jnp.concatenate(result, axis=0)


def project_kernel(offset, core_ref, own_ref, *refs):
    cores, slots = len(offset), len(offset[0])
    moved_refs, w_refs = refs[:slots], refs[slots : slots + cores]
    out_refs = refs[slots + cores : 2 * slots + cores]
    left = take_slots(offset, core_ref, own_ref, moved_refs)
    rows, part = own_ref.shape[0], w_refs[0].shape[1]
    for j in range(cores):
        product = jnp.dot(left, w_refs[j][...], preferred_element_type=F32).astype(BF16)
        for s in range(slots):
            out_refs[s][:, j * part : (j + 1) * part] = product[s * rows : (s + 1) * rows]


def project(place, own, moved, weights, offset):
    rows = own.shape[0]
    depth, part = weights[0].shape
    cores, slots = len(offset), len(offset[0])
    return pl.pallas_call(
        functools.partial(project_kernel, offset),
        out_shape=[jax.ShapeDtypeStruct((rows, part * cores), BF16)] * slots,
        in_specs=[SMEM, VMEM] + [VMEM] * (slots + cores),
        out_specs=[VMEM] * slots,
        compiler_params=pltpu.CompilerParams(vmem_limit_bytes=12 * MIB),
    )(place[1], own, *moved, *weights)


def norm_kernel(cores, experts, core_ref, *refs):
    sums_refs, stream_refs, gain_refs = refs[:cores], refs[cores : 2 * cores], refs[2 * cores : 3 * cores]
    ids_ref, routes_ref, mixed_ref, out_ref = refs[3 * cores :]
    rows, part = stream_refs[0].shape
    width = part * cores
    core = core_ref[0]
    squares = 0.0
    mixed = []
    for j in range(cores):
        block = from_natural(core, stream_refs[j][...].astype(F32), cores)
        for m in range(cores):
            other = sums_refs[m][:, (j ^ m) * part : ((j ^ m) + 1) * part]
            block = block + turned(other, m, cores)
        mixed.append(block)
        squares = squares + jnp.sum(block * block, axis=1, keepdims=True)
    mixed_ref[...] = mixed[0]
    scale = lax.rsqrt(squares / width + 1e-06)
    for j in range(cores):
        out_ref[:, j * part : (j + 1) * part] = (mixed[j] * scale * gain_refs[j][...]).astype(BF16)
    picks = ids_ref.shape[0]
    extra = out_ref.shape[1] - width
    ids, routes = ids_ref[...], routes_ref[...]
    shares = routes / jnp.sum(routes, axis=0, keepdims=True)
    line = lax.broadcasted_iota(jnp.int32, (extra, rows), 0)
    line = jnp.where(line < experts, line, line - experts)
    combine = jnp.zeros((extra, rows), F32)
    for k in range(picks):
        combine = jnp.where(ids[k : k + 1, :] == line, shares[k : k + 1, :], combine)
    combine = jnp.concatenate([combine, jnp.zeros((extra, 128 - rows), F32)], axis=1)
    combine = from_natural(core, jnp.transpose(combine)[:rows], cores)
    upper = combine.astype(BF16)
    lower = (combine - upper.astype(F32)).astype(BF16)
    lane = lax.broadcasted_iota(jnp.int32, (rows, extra), 1)
    out_ref[:, width:] = jnp.where(lane < experts, upper.astype(F32), lower.astype(F32)).astype(BF16)


def normalise(place, sums, stream, gain, ids, routes, experts):
    rows, part = stream[0].shape
    cores = len(sums)
    extra = -(-2 * experts // 128) * 128
    return pl.pallas_call(
        functools.partial(norm_kernel, cores, experts),
        out_shape=(
            jax.ShapeDtypeStruct((rows, part), F32),
            jax.ShapeDtypeStruct((rows, part * cores + extra), BF16),
        ),
        in_specs=[SMEM] + [VMEM] * (3 * cores + 2),
        out_specs=(VMEM, VMEM),
        compiler_params=pltpu.CompilerParams(vmem_limit_bytes=8 * MIB),
    )(place[1], *sums, *stream, *gain, ids.T, routes.T)


def fetch_kernel(count, *refs):
    sources, targets, sems = refs[:count], refs[count : 2 * count], refs[2 * count]
    copies = [
        pltpu.make_async_copy(sources[i].at[0], targets[i], sems.at[i]) for i in range(count)
    ]
    for copy in copies:
        copy.start()
    for copy in copies:
        copy.wait()


def fetch(weights):
    count = len(weights)
    return pl.pallas_call(
        functools.partial(fetch_kernel, count),
        out_shape=[jax.ShapeDtypeStruct(w.shape[1:], w.dtype) for w in weights],
        in_specs=[ANY] * count,
        out_specs=[VMEM] * count,
        scratch_shapes=[pltpu.SemaphoreType.DMA((count,))],
        compiler_params=pltpu.CompilerParams(vmem_limit_bytes=42 * MIB),
    )(*weights)


def expert_kernel(offset, devs, me_ref, core_ref, own_ref, *refs):
    cores, slots = len(offset), len(offset[0])
    moved_refs, refs = refs[:slots], refs[slots:]
    first_refs, refs = refs[: 3 * cores], refs[3 * cores :]
    weight_refs = refs[: 3 * cores]
    out_refs = refs[3 * cores : 3 * cores + slots]
    gate_buf, up_buf, down_buf, sems = refs[3 * cores + slots :]
    local, part, hidden = weight_refs[0].shape
    rows = own_ref.shape[0]
    width = part * cores
    bufs = (gate_buf, up_buf, down_buf)

    def copy(kind, j, e):
        return pltpu.make_async_copy(
            weight_refs[kind * cores + j].at[e], bufs[kind].at[j, e - 1], sems.at[kind, j, e - 1]
        )

    def weight(kind, j, e):
        if e == 0:
            return first_refs[kind * cores + j][...]
        copy(kind, j, e).wait()
        return bufs[kind][j, e - 1]

    for e in range(1, local):
        for kind in range(3):
            for j in range(cores):
                copy(kind, j, e).start()
    tokens = take_slots(offset, core_ref, own_ref, moved_refs)
    tail = tokens[:, width:].astype(F32)
    lane = lax.broadcasted_iota(jnp.int32, tail.shape, 1)
    experts = local * devs
    total = [0.0] * cores
    for e in range(local):
        mine = me_ref[0] * local + e
        share = jnp.sum(
            jnp.where((lane == mine) | (lane == mine + experts), tail, 0.0), axis=1, keepdims=True
        )
        sums = []
        for kind in range(2):
            value = 0.0
            for j in range(cores):
                value = value + jnp.dot(
                    tokens[:, j * part : (j + 1) * part],
                    weight(kind, j, e),
                    preferred_element_type=F32,
                )
            sums.append(value)
        gate, up = sums
        active = (gate / (1.0 + jnp.exp(-gate)) * up * share).astype(BF16)
        for j in range(cores):
            total[j] = total[j] + jnp.dot(active, weight(2, j, e), preferred_element_type=F32)
    for j in range(cores):
        for s in range(slots):
            out_refs[s][:, j * part : (j + 1) * part] = total[j][
                s * rows : (s + 1) * rows
            ].astype(BF16)


def apply_experts(place, own, moved, first, weights, offset, devs):
    cores, slots = len(offset), len(offset[0])
    local, part, hidden = weights[0].shape
    rows = own.shape[0]
    return pl.pallas_call(
        functools.partial(expert_kernel, offset, devs),
        out_shape=[jax.ShapeDtypeStruct((rows, part * cores), BF16)] * slots,
        in_specs=[SMEM, SMEM, VMEM] + [VMEM] * (slots + 3 * cores) + [ANY] * (3 * cores),
        out_specs=[VMEM] * slots,
        scratch_shapes=[
            pltpu.VMEM((cores, local - 1, part, hidden), BF16),
            pltpu.VMEM((cores, local - 1, part, hidden), BF16),
            pltpu.VMEM((cores, local - 1, hidden, part), BF16),
            pltpu.SemaphoreType.DMA((3, cores, local - 1)),
        ],
        compiler_params=pltpu.CompilerParams(vmem_limit_bytes=42 * MIB),
    )(*place, own, *moved, *first, *weights)


def per_device(
    query,
    stored_keys,
    stored_values,
    incoming_key,
    incoming_value,
    lengths,
    out_weight,
    residual,
    norm_gain,
    expert_ids,
    route_weights,
    w_gate,
    w_up,
    w_down,
):
    devs = lax.axis_size("dev")
    cores = lax.axis_size("pair")
    me = lax.axis_index("dev")
    core = lax.axis_index("pair")
    slots = devs // cores
    offset = TUNED.get(
        (devs, cores), [[c * slots + s for s in range(slots)] for c in range(cores)]
    )
    place = (me.astype(jnp.int32).reshape(1), core.astype(jnp.int32).reshape(1))
    rows, part = residual.shape
    barrier = lax.optimization_barrier

    def from_core(value, m):
        return lax.ppermute(value, "pair", [(c, c ^ m) for c in range(cores)])

    def gathered(value):
        return [value] + [from_core(value, m) for m in range(1, cores)]

    def swap(value, s):
        pairs = [
            (d * cores + c, (d ^ offset[c][s]) * cores + c)
            for d in range(devs)
            for c in range(cores)
            if offset[c][s]
        ]
        return lax.ppermute(value, ("dev", "pair"), pairs)

    own_slot = [[c for c in range(cores) if offset[c][s] == 0] for s in range(slots)]

    def total_of(own, moved):
        result = 0.0
        for s in (2, 3, 0, 1):
            block = moved[s]
            for c in own_slot[s]:
                block = jnp.where(core == c, own[s], block)
            result = result + block.astype(F32)
        return result

    def own_block(blocks):
        return blocks[[s for s in range(slots) if own_slot[s]][0]]

    stream = gathered(residual)
    gain = gathered(norm_gain.reshape(1, part))
    wg = gathered(w_gate)
    attended = attend(
        query, stored_keys, stored_values, incoming_key, incoming_value, lengths, place, offset
    )
    attended, wg, stream, gain = barrier((attended, wg, stream, gain))
    held = [attended[0]] + [from_core(attended[m], m) for m in range(1, cores)]
    held, out_weight, w_up, w_down = barrier((held, out_weight, w_up, w_down))
    wo = gathered(out_weight)
    outgoing = [jnp.concatenate([h[s] for h in held], axis=0) for s in range(slots)]
    arrived = [swap(outgoing[s], s) for s in range(slots)]
    arrived, wo, w_up, w_down = barrier((arrived, wo, w_up, w_down))
    wu = gathered(w_up)
    partial = project(place, own_block(outgoing), arrived, wo, offset)
    sums = total_of(partial, [swap(partial[s], s) for s in range(slots)])
    sums, wu, w_down = barrier((sums, wu, w_down))
    mixed, packed = normalise(
        place, gathered(sums), stream, gain, expert_ids, route_weights, w_gate.shape[0] * devs
    )
    packed, weights, w_down = barrier((packed, wg + wu, w_down))
    tokens = [swap(packed, s) for s in range(slots)]
    weights = weights + gathered(w_down)
    first = fetch(weights)
    produced = apply_experts(place, packed, tokens, first, weights, offset, devs)
    back = total_of(produced, [swap(produced[s], s) for s in range(slots)])
    result = mixed + back[:, :part]
    for m in range(1, cores):
        other = from_core(back[:, m * part : (m + 1) * part], m)
        result = result + turned(other, m, cores)
    return from_natural(core, result, cores).astype(BF16)


def solution(mesh):
    in_specs = (
        P(("groups", "dev", "pair"), None, None),
        P(("groups", "dev", "pair"), None, None, None),
        P(("groups", "dev", "pair"), None, None, None),
        P(("groups", "dev", "pair"), None, None),
        P(("groups", "dev", "pair"), None, None),
        P(("groups", "dev", "pair")),
        P("dev", "pair"),
        P(("groups", "dev"), "pair"),
        P("pair"),
        P(("groups", "dev"), None),
        P(("groups", "dev"), None),
        P("dev", "pair", None),
        P("dev", "pair", None),
        P("dev", None, "pair"),
    )
    out_specs = P(("groups", "dev"), "pair")
    return jax.shard_map(
        per_device, mesh=mesh, in_specs=in_specs, out_specs=out_specs, check_vma=False
    )
```

```python
import functools
import math

import jax
import jax.numpy as jnp
from jax import lax
from jax.experimental import pallas as pl
from jax.experimental.pallas import tpu as pltpu
from jax.sharding import PartitionSpec as P

F32 = jnp.float32
BF16 = jnp.bfloat16
VMEM = pl.BlockSpec(memory_space=pltpu.VMEM)
SMEM = pl.BlockSpec(memory_space=pltpu.SMEM)
ANY = pl.BlockSpec(memory_space=pl.ANY)
MIB = 1024 * 1024
TUNED = {(8, 2): ((5, 0, 3, 6), (7, 1, 2, 4))}


def choose(core, values):
    result = jnp.int32(values[0])
    for c in range(1, len(values)):
        result = jnp.where(core == c, jnp.int32(values[c]), result)
    return result


def turned(value, m, cores):
    band = value.shape[0] // cores
    pieces = [value[i * band : (i + 1) * band] for i in range(cores)]
    return jnp.concatenate([pieces[i ^ m] for i in range(cores)], axis=0) if m else value


def from_natural(core, value, cores):
    result = value
    for c in range(1, cores):
        result = jnp.where(core == c, turned(value, c, cores), result)
    return result


def attend_kernel(
    kv_heads, offset, len_ref, me_ref, core_ref, q_hbm, k_hbm, v_hbm, ik_hbm, iv_hbm, *refs
):
    cores, slots = len(offset), len(offset[0])
    out_refs = refs[:cores]
    q_ref, ik_ref, iv_ref, k_buf, v_buf, mask_ref, all_ref, order_ref, sems, small_sems = refs[cores:]
    rows, heads, size = q_ref.shape
    span = k_buf.shape[1]
    per = heads // kv_heads
    block = heads // (cores * slots)
    scale = size ** (-0.5) * math.log2(math.e)
    step = 4
    chunks = 4
    chunk = span // chunks

    small = [
        pltpu.make_async_copy(source, target, small_sems.at[n])
        for n, (source, target) in enumerate(
            ((q_hbm, q_ref), (ik_hbm, ik_ref), (iv_hbm, iv_ref))
        )
    ]
    for copy in small:
        copy.start()

    lengths = [len_ref[r] for r in range(rows)]
    ranks = [jnp.int32(0)] * rows
    for i in range(rows):
        for j in range(i + 1, rows):
            later = (lengths[i] < lengths[j]).astype(jnp.int32)
            ranks[i] = ranks[i] + later
            ranks[j] = ranks[j] + (1 - later)
    for r in range(rows):
        order_ref[ranks[r]] = jnp.int32(r)

    def copies(i, used):
        r = order_ref[i]
        part = pl.ds(0, used)
        return (
            pltpu.make_async_copy(k_hbm.at[r, part], k_buf.at[r, part], sems.at[0, i]),
            pltpu.make_async_copy(v_hbm.at[r, part], v_buf.at[r, part], sems.at[1, i]),
        )

    def by_length(i, work):
        needed = (len_ref[order_ref[i * step]] * kv_heads + (chunk - 1)) // chunk
        for n in range(1, chunks + 1):

            @pl.when(needed == n)
            def _():
                work(n * chunk)

    def begin(i, carry):
        def work(used):
            for j in range(step):
                for copy in copies(i * step + j, used):
                    copy.start()

        by_length(i, work)
        return carry

    lax.fori_loop(0, rows // step, begin, 0)
    column = lax.broadcasted_iota(jnp.int32, (heads, span), 1)
    head = lax.broadcasted_iota(jnp.int32, (heads, span), 0)
    mask_ref[...] = jnp.where((column & (kv_heads - 1)) == (head >> (per.bit_length() - 1)), column, 1 << 30)

    def spread(value):
        return jnp.concatenate(
            [
                jnp.broadcast_to(value[g : g + 1, :].astype(F32), (per, size))
                for g in range(kv_heads)
            ],
            axis=0,
        )

    def several(group, used):
        queries = [q_ref[r] for r in group]
        scores = [
            lax.dot_general(
                q, k_buf[r, :used], (((1,), (1,)), ((), ())), preferred_element_type=F32
            )
            for q, r in zip(queries, group)
        ]
        own = [
            jnp.sum(q.astype(F32) * spread(ik_ref[r]), axis=1, keepdims=True)
            for q, r in zip(queries, group)
        ]
        scores = [
            jnp.where(mask_ref[:, :used] < len_ref[r] * kv_heads, x, -1e30)
            for x, r in zip(scores, group)
        ]
        peak = [
            jnp.maximum(jnp.max(x, axis=1, keepdims=True), o) for x, o in zip(scores, own)
        ]
        expo = [jnp.exp2((x - p) * scale) for x, p in zip(scores, peak)]
        accum = [
            jnp.dot(x.astype(BF16), v_buf[r, :used], preferred_element_type=F32)
            for x, r in zip(expo, group)
        ]
        fresh = [jnp.exp2((o - p) * scale) for o, p in zip(own, peak)]
        total = [jnp.sum(x, axis=1, keepdims=True) + f for x, f in zip(expo, fresh)]
        for x, f, t, r in zip(accum, fresh, total, group):
            all_ref[pl.ds(r, heads, stride=rows), :] = (x + f * spread(iv_ref[r])) / t

    def body(i, carry):
        def work(used):
            for j in range(step):
                for copy in copies(i * step + j, used):
                    copy.wait()
            several([order_ref[i * step + j] for j in range(step)], used)

        by_length(i, work)
        return carry

    for copy in small:
        copy.wait()
    lax.fori_loop(0, rows // step, body, 0)
    me, core = me_ref[0], core_ref[0]
    for m in range(cores):
        for s in range(slots):
            which = me ^ choose(core, [offset[c ^ m][s] for c in range(cores)])
            for h in range(block):
                at = pl.multiple_of((which * block + h) * rows, rows)
                out_refs[m][s, :, h * size : (h + 1) * size] = all_ref[
                    pl.ds(at, rows), :
                ].astype(BF16)


def attend(query, keys, values, fresh_key, fresh_value, lengths, place, offset):
    rows, heads, size = query.shape
    positions, kv_heads = keys.shape[1:3]
    span = positions * kv_heads
    cores, slots = len(offset), len(offset[0])
    width = heads * size // (cores * slots)
    return pl.pallas_call(
        functools.partial(attend_kernel, kv_heads, offset),
        out_shape=[jax.ShapeDtypeStruct((slots, rows, width), BF16)] * cores,
        in_specs=[SMEM, SMEM, SMEM] + [ANY] * 5,
        out_specs=[VMEM] * cores,
        scratch_shapes=[
            pltpu.VMEM(query.shape, BF16),
            pltpu.VMEM(fresh_key.shape, BF16),
            pltpu.VMEM(fresh_value.shape, BF16),
            pltpu.VMEM((rows, span, size), BF16),
            pltpu.VMEM((rows, span, size), BF16),
            pltpu.VMEM((heads, span), jnp.int32),
            pltpu.VMEM((heads * rows, size), F32),
            pltpu.SMEM((rows,), jnp.int32),
            pltpu.SemaphoreType.DMA((2, rows)),
            pltpu.SemaphoreType.DMA((3,)),
        ],
        compiler_params=pltpu.CompilerParams(vmem_limit_bytes=60 * MIB),
    )(
        lengths,
        *place,
        query,
        keys.reshape(rows, span, size),
        values.reshape(rows, span, size),
        fresh_key,
        fresh_value,
    )


def take_slots(offset, core_ref, own_ref, moved_refs):
    core = core_ref[0]
    result = []
    for s, ref in enumerate(moved_refs):
        block = ref[...]
        for c in range(len(offset)):
            if offset[c][s] == 0:
                block = jnp.where(core == c, own_ref[...], block)
        result.append(block)
    return jnp.concatenate(result, axis=0)


def project_kernel(offset, core_ref, own_ref, *refs):
    cores, slots = len(offset), len(offset[0])
    moved_refs, w_refs = refs[:slots], refs[slots : slots + cores]
    out_refs = refs[slots + cores : 2 * slots + cores]
    left = take_slots(offset, core_ref, own_ref, moved_refs)
    rows, part = own_ref.shape[0], w_refs[0].shape[1]
    for j in range(cores):
        product = jnp.dot(left, w_refs[j][...], preferred_element_type=F32).astype(BF16)
        for s in range(slots):
            out_refs[s][:, j * part : (j + 1) * part] = product[s * rows : (s + 1) * rows]


def project(place, own, moved, weights, offset):
    rows = own.shape[0]
    depth, part = weights[0].shape
    cores, slots = len(offset), len(offset[0])
    return pl.pallas_call(
        functools.partial(project_kernel, offset),
        out_shape=[jax.ShapeDtypeStruct((rows, part * cores), BF16)] * slots,
        in_specs=[SMEM, VMEM] + [VMEM] * (slots + cores),
        out_specs=[VMEM] * slots,
        compiler_params=pltpu.CompilerParams(vmem_limit_bytes=12 * MIB),
    )(place[1], own, *moved, *weights)


def norm_kernel(cores, experts, core_ref, *refs):
    sums_refs, stream_refs, gain_refs = refs[:cores], refs[cores : 2 * cores], refs[2 * cores : 3 * cores]
    ids_ref, routes_ref, mixed_ref, out_ref = refs[3 * cores :]
    rows, part = stream_refs[0].shape
    width = part * cores
    core = core_ref[0]
    squares = 0.0
    mixed = []
    for j in range(cores):
        block = from_natural(core, stream_refs[j][...].astype(F32), cores)
        for m in range(cores):
            other = sums_refs[m][:, (j ^ m) * part : ((j ^ m) + 1) * part]
            block = block + turned(other, m, cores)
        mixed.append(block)
        squares = squares + jnp.sum(block * block, axis=1, keepdims=True)
    mixed_ref[...] = mixed[0]
    scale = lax.rsqrt(squares / width + 1e-06)
    for j in range(cores):
        out_ref[:, j * part : (j + 1) * part] = (mixed[j] * scale * gain_refs[j][...]).astype(BF16)
    picks = ids_ref.shape[0]
    extra = out_ref.shape[1] - width
    ids, routes = ids_ref[...], routes_ref[...]
    shares = routes / jnp.sum(routes, axis=0, keepdims=True)
    line = lax.broadcasted_iota(jnp.int32, (extra, rows), 0)
    line = jnp.where(line < experts, line, line - experts)
    combine = jnp.zeros((extra, rows), F32)
    for k in range(picks):
        combine = jnp.where(ids[k : k + 1, :] == line, shares[k : k + 1, :], combine)
    combine = jnp.concatenate([combine, jnp.zeros((extra, 128 - rows), F32)], axis=1)
    combine = from_natural(core, jnp.transpose(combine)[:rows], cores)
    upper = combine.astype(BF16)
    lower = (combine - upper.astype(F32)).astype(BF16)
    lane = lax.broadcasted_iota(jnp.int32, (rows, extra), 1)
    out_ref[:, width:] = jnp.where(lane < experts, upper.astype(F32), lower.astype(F32)).astype(BF16)


def normalise(place, sums, stream, gain, ids, routes, experts):
    rows, part = stream[0].shape
    cores = len(sums)
    extra = -(-2 * experts // 128) * 128
    return pl.pallas_call(
        functools.partial(norm_kernel, cores, experts),
        out_shape=(
            jax.ShapeDtypeStruct((rows, part), F32),
            jax.ShapeDtypeStruct((rows, part * cores + extra), BF16),
        ),
        in_specs=[SMEM] + [VMEM] * (3 * cores + 2),
        out_specs=(VMEM, VMEM),
        compiler_params=pltpu.CompilerParams(vmem_limit_bytes=8 * MIB),
    )(place[1], *sums, *stream, *gain, ids.T, routes.T)


def fetch_kernel(count, *refs):
    sources, targets, sems = refs[:count], refs[count : 2 * count], refs[2 * count]
    copies = [
        pltpu.make_async_copy(sources[i].at[0], targets[i], sems.at[i]) for i in range(count)
    ]
    for copy in copies:
        copy.start()
    for copy in copies:
        copy.wait()


def fetch(weights):
    count = len(weights)
    return pl.pallas_call(
        functools.partial(fetch_kernel, count),
        out_shape=[jax.ShapeDtypeStruct(w.shape[1:], w.dtype) for w in weights],
        in_specs=[ANY] * count,
        out_specs=[VMEM] * count,
        scratch_shapes=[pltpu.SemaphoreType.DMA((count,))],
        compiler_params=pltpu.CompilerParams(vmem_limit_bytes=42 * MIB),
    )(*weights)


def expert_kernel(offset, devs, me_ref, core_ref, own_ref, *refs):
    cores, slots = len(offset), len(offset[0])
    moved_refs, refs = refs[:slots], refs[slots:]
    first_refs, refs = refs[: 3 * cores], refs[3 * cores :]
    weight_refs = refs[: 3 * cores]
    out_refs = refs[3 * cores : 3 * cores + slots]
    gate_buf, up_buf, down_buf, sems = refs[3 * cores + slots :]
    local, part, hidden = weight_refs[0].shape
    rows = own_ref.shape[0]
    width = part * cores
    bufs = (gate_buf, up_buf, down_buf)

    def copy(kind, j, e):
        return pltpu.make_async_copy(
            weight_refs[kind * cores + j].at[e], bufs[kind].at[j, e - 1], sems.at[kind, j, e - 1]
        )

    def weight(kind, j, e):
        if e == 0:
            return first_refs[kind * cores + j][...]
        copy(kind, j, e).wait()
        return bufs[kind][j, e - 1]

    for e in range(1, local):
        for kind in range(3):
            for j in range(cores):
                copy(kind, j, e).start()
    tokens = take_slots(offset, core_ref, own_ref, moved_refs)
    tail = tokens[:, width:].astype(F32)
    lane = lax.broadcasted_iota(jnp.int32, tail.shape, 1)
    experts = local * devs
    total = [0.0] * cores
    for e in range(local):
        mine = me_ref[0] * local + e
        share = jnp.sum(
            jnp.where((lane == mine) | (lane == mine + experts), tail, 0.0), axis=1, keepdims=True
        )
        sums = []
        for kind in range(2):
            value = 0.0
            for j in range(cores):
                value = value + jnp.dot(
                    tokens[:, j * part : (j + 1) * part],
                    weight(kind, j, e),
                    preferred_element_type=F32,
                )
            sums.append(value)
        gate, up = sums
        active = (gate / (1.0 + jnp.exp(-gate)) * up * share).astype(BF16)
        for j in range(cores):
            total[j] = total[j] + jnp.dot(active, weight(2, j, e), preferred_element_type=F32)
    for j in range(cores):
        for s in range(slots):
            out_refs[s][:, j * part : (j + 1) * part] = total[j][
                s * rows : (s + 1) * rows
            ].astype(BF16)


def apply_experts(place, own, moved, first, weights, offset, devs):
    cores, slots = len(offset), len(offset[0])
    local, part, hidden = weights[0].shape
    rows = own.shape[0]
    return pl.pallas_call(
        functools.partial(expert_kernel, offset, devs),
        out_shape=[jax.ShapeDtypeStruct((rows, part * cores), BF16)] * slots,
        in_specs=[SMEM, SMEM, VMEM] + [VMEM] * (slots + 3 * cores) + [ANY] * (3 * cores),
        out_specs=[VMEM] * slots,
        scratch_shapes=[
            pltpu.VMEM((cores, local - 1, part, hidden), BF16),
            pltpu.VMEM((cores, local - 1, part, hidden), BF16),
            pltpu.VMEM((cores, local - 1, hidden, part), BF16),
            pltpu.SemaphoreType.DMA((3, cores, local - 1)),
        ],
        compiler_params=pltpu.CompilerParams(vmem_limit_bytes=42 * MIB),
    )(*place, own, *moved, *first, *weights)


def per_device(
    query,
    stored_keys,
    stored_values,
    incoming_key,
    incoming_value,
    lengths,
    out_weight,
    residual,
    norm_gain,
    expert_ids,
    route_weights,
    w_gate,
    w_up,
    w_down,
):
    devs = lax.axis_size("dev")
    cores = lax.axis_size("pair")
    me = lax.axis_index("dev")
    core = lax.axis_index("pair")
    slots = devs // cores
    offset = TUNED.get(
        (devs, cores), [[c * slots + s for s in range(slots)] for c in range(cores)]
    )
    place = (me.astype(jnp.int32).reshape(1), core.astype(jnp.int32).reshape(1))
    rows, part = residual.shape
    barrier = lax.optimization_barrier

    def from_core(value, m):
        return lax.ppermute(value, "pair", [(c, c ^ m) for c in range(cores)])

    def gathered(value):
        return [value] + [from_core(value, m) for m in range(1, cores)]

    def swap(value, s):
        pairs = [
            (d * cores + c, (d ^ offset[c][s]) * cores + c)
            for d in range(devs)
            for c in range(cores)
            if offset[c][s]
        ]
        return lax.ppermute(value, ("dev", "pair"), pairs)

    own_slot = [[c for c in range(cores) if offset[c][s] == 0] for s in range(slots)]

    def total_of(own, moved):
        result = 0.0
        for s in (2, 3, 0, 1):
            block = moved[s]
            for c in own_slot[s]:
                block = jnp.where(core == c, own[s], block)
            result = result + block.astype(F32)
        return result

    def own_block(blocks):
        return blocks[[s for s in range(slots) if own_slot[s]][0]]

    stream = gathered(residual)
    gain = gathered(norm_gain.reshape(1, part))
    wg = gathered(w_gate)
    attended = attend(
        query, stored_keys, stored_values, incoming_key, incoming_value, lengths, place, offset
    )
    attended, wg, stream, gain = barrier((attended, wg, stream, gain))
    mine = barrier([attended[0][s] for s in range(slots)])
    theirs = [from_core(attended[m], m) for m in range(1, cores)]
    outgoing = [
        jnp.concatenate([mine[s]] + [block[s] for block in theirs], axis=0) for s in range(slots)
    ]
    outgoing, out_weight, w_up, w_down = barrier((outgoing, out_weight, w_up, w_down))
    wo = gathered(out_weight)
    arrived = [swap(outgoing[s], s) for s in range(slots)]
    arrived, wo, w_up, w_down = barrier((arrived, wo, w_up, w_down))
    wu = gathered(w_up)
    partial = project(place, own_block(outgoing), arrived, wo, offset)
    sums = total_of(partial, [swap(partial[s], s) for s in range(slots)])
    sums, wu, w_down = barrier((sums, wu, w_down))
    mixed, packed = normalise(
        place, gathered(sums), stream, gain, expert_ids, route_weights, w_gate.shape[0] * devs
    )
    packed, weights, w_down = barrier((packed, wg + wu, w_down))
    tokens = [swap(packed, s) for s in range(slots)]
    weights = weights + gathered(w_down)
    first = fetch(weights)
    produced = apply_experts(place, packed, tokens, first, weights, offset, devs)
    back = total_of(produced, [swap(produced[s], s) for s in range(slots)])
    result = mixed + back[:, :part]
    for m in range(1, cores):
        other = from_core(back[:, m * part : (m + 1) * part], m)
        result = result + turned(other, m, cores)
    return from_natural(core, result, cores).astype(BF16)


def solution(mesh):
    in_specs = (
        P(("groups", "dev", "pair"), None, None),
        P(("groups", "dev", "pair"), None, None, None),
        P(("groups", "dev", "pair"), None, None, None),
        P(("groups", "dev", "pair"), None, None),
        P(("groups", "dev", "pair"), None, None),
        P(("groups", "dev", "pair")),
        P("dev", "pair"),
        P(("groups", "dev"), "pair"),
        P("pair"),
        P(("groups", "dev"), None),
        P(("groups", "dev"), None),
        P("dev", "pair", None),
        P("dev", "pair", None),
        P("dev", None, "pair"),
    )
    out_specs = P(("groups", "dev"), "pair")
    return jax.shard_map(
        per_device, mesh=mesh, in_specs=in_specs, out_specs=out_specs, check_vma=False
    )
```

```python
import functools
import math

import jax
import jax.numpy as jnp
from jax import lax
from jax.experimental import pallas as pl
from jax.experimental.pallas import tpu as pltpu
from jax.sharding import PartitionSpec as P

F32 = jnp.float32
BF16 = jnp.bfloat16
VMEM = pl.BlockSpec(memory_space=pltpu.VMEM)
SMEM = pl.BlockSpec(memory_space=pltpu.SMEM)
ANY = pl.BlockSpec(memory_space=pl.ANY)
MIB = 1024 * 1024
TUNED = {(8, 2): ((5, 0, 3, 6), (7, 1, 4, 2))}


def choose(core, values):
    result = jnp.int32(values[0])
    for c in range(1, len(values)):
        result = jnp.where(core == c, jnp.int32(values[c]), result)
    return result


def turned(value, m, cores):
    band = value.shape[0] // cores
    pieces = [value[i * band : (i + 1) * band] for i in range(cores)]
    return jnp.concatenate([pieces[i ^ m] for i in range(cores)], axis=0) if m else value


def from_natural(core, value, cores):
    result = value
    for c in range(1, cores):
        result = jnp.where(core == c, turned(value, c, cores), result)
    return result


def attend_kernel(
    kv_heads, offset, len_ref, me_ref, core_ref, q_hbm, k_hbm, v_hbm, ik_hbm, iv_hbm, *refs
):
    cores, slots = len(offset), len(offset[0])
    out_refs = refs[:cores]
    q_ref, ik_ref, iv_ref, k_buf, v_buf, mask_ref, all_ref, order_ref, sems, small_sems = refs[cores:]
    rows, heads, size = q_ref.shape
    span = k_buf.shape[1]
    per = heads // kv_heads
    block = heads // (cores * slots)
    scale = size ** (-0.5) * math.log2(math.e)
    step = 4
    chunks = 4
    chunk = span // chunks

    small = [
        pltpu.make_async_copy(source, target, small_sems.at[n])
        for n, (source, target) in enumerate(
            ((q_hbm, q_ref), (ik_hbm, ik_ref), (iv_hbm, iv_ref))
        )
    ]
    for copy in small:
        copy.start()

    lengths = [len_ref[r] for r in range(rows)]
    ranks = [jnp.int32(0)] * rows
    for i in range(rows):
        for j in range(i + 1, rows):
            later = (lengths[i] < lengths[j]).astype(jnp.int32)
            ranks[i] = ranks[i] + later
            ranks[j] = ranks[j] + (1 - later)
    for r in range(rows):
        order_ref[ranks[r]] = jnp.int32(r)

    def copies(i, used):
        r = order_ref[i]
        part = pl.ds(0, used)
        return (
            pltpu.make_async_copy(k_hbm.at[r, part], k_buf.at[r, part], sems.at[0, i]),
            pltpu.make_async_copy(v_hbm.at[r, part], v_buf.at[r, part], sems.at[1, i]),
        )

    def by_length(i, work):
        needed = (len_ref[order_ref[i * step]] * kv_heads + (chunk - 1)) // chunk
        for n in range(1, chunks + 1):

            @pl.when(needed == n)
            def _():
                work(n * chunk)

    def begin(i, carry):
        def work(used):
            for j in range(step):
                for copy in copies(i * step + j, used):
                    copy.start()

        by_length(i, work)
        return carry

    lax.fori_loop(0, rows // step, begin, 0)
    column = lax.broadcasted_iota(jnp.int32, (heads, span), 1)
    head = lax.broadcasted_iota(jnp.int32, (heads, span), 0)
    mask_ref[...] = jnp.where((column & (kv_heads - 1)) == (head >> (per.bit_length() - 1)), column, 1 << 30)

    def spread(value):
        return jnp.concatenate(
            [
                jnp.broadcast_to(value[g : g + 1, :].astype(F32), (per, size))
                for g in range(kv_heads)
            ],
            axis=0,
        )

    def several(group, used):
        queries = [q_ref[r] for r in group]
        scores = [
            lax.dot_general(
                q, k_buf[r, :used], (((1,), (1,)), ((), ())), preferred_element_type=F32
            )
            for q, r in zip(queries, group)
        ]
        own = [
            jnp.sum(q.astype(F32) * spread(ik_ref[r]), axis=1, keepdims=True)
            for q, r in zip(queries, group)
        ]
        scores = [
            jnp.where(mask_ref[:, :used] < len_ref[r] * kv_heads, x, -1e30)
            for x, r in zip(scores, group)
        ]
        peak = [
            jnp.maximum(jnp.max(x, axis=1, keepdims=True), o) for x, o in zip(scores, own)
        ]
        expo = [jnp.exp2((x - p) * scale) for x, p in zip(scores, peak)]
        accum = [
            jnp.dot(x.astype(BF16), v_buf[r, :used], preferred_element_type=F32)
            for x, r in zip(expo, group)
        ]
        fresh = [jnp.exp2((o - p) * scale) for o, p in zip(own, peak)]
        total = [jnp.sum(x, axis=1, keepdims=True) + f for x, f in zip(expo, fresh)]
        for x, f, t, r in zip(accum, fresh, total, group):
            all_ref[pl.ds(r, heads, stride=rows), :] = (x + f * spread(iv_ref[r])) / t

    def body(i, carry):
        def work(used):
            for j in range(step):
                for copy in copies(i * step + j, used):
                    copy.wait()
            several([order_ref[i * step + j] for j in range(step)], used)

        by_length(i, work)
        return carry

    for copy in small:
        copy.wait()
    lax.fori_loop(0, rows // step, body, 0)
    me, core = me_ref[0], core_ref[0]
    for m in range(cores):
        for s in range(slots):
            which = me ^ choose(core, [offset[c ^ m][s] for c in range(cores)])
            for h in range(block):
                at = pl.multiple_of((which * block + h) * rows, rows)
                out_refs[m][s, :, h * size : (h + 1) * size] = all_ref[
                    pl.ds(at, rows), :
                ].astype(BF16)


def attend(query, keys, values, fresh_key, fresh_value, lengths, place, offset):
    rows, heads, size = query.shape
    positions, kv_heads = keys.shape[1:3]
    span = positions * kv_heads
    cores, slots = len(offset), len(offset[0])
    width = heads * size // (cores * slots)
    return pl.pallas_call(
        functools.partial(attend_kernel, kv_heads, offset),
        out_shape=[jax.ShapeDtypeStruct((slots, rows, width), BF16)] * cores,
        in_specs=[SMEM, SMEM, SMEM] + [ANY] * 5,
        out_specs=[VMEM] * cores,
        scratch_shapes=[
            pltpu.VMEM(query.shape, BF16),
            pltpu.VMEM(fresh_key.shape, BF16),
            pltpu.VMEM(fresh_value.shape, BF16),
            pltpu.VMEM((rows, span, size), BF16),
            pltpu.VMEM((rows, span, size), BF16),
            pltpu.VMEM((heads, span), jnp.int32),
            pltpu.VMEM((heads * rows, size), F32),
            pltpu.SMEM((rows,), jnp.int32),
            pltpu.SemaphoreType.DMA((2, rows)),
            pltpu.SemaphoreType.DMA((3,)),
        ],
        compiler_params=pltpu.CompilerParams(vmem_limit_bytes=60 * MIB),
    )(
        lengths,
        *place,
        query,
        keys.reshape(rows, span, size),
        values.reshape(rows, span, size),
        fresh_key,
        fresh_value,
    )


def take_slots(offset, core_ref, own_ref, moved_refs):
    core = core_ref[0]
    result = []
    for s, ref in enumerate(moved_refs):
        block = ref[...]
        for c in range(len(offset)):
            if offset[c][s] == 0:
                block = jnp.where(core == c, own_ref[...], block)
        result.append(block)
    return jnp.concatenate(result, axis=0)


def project_kernel(offset, core_ref, own_ref, *refs):
    cores, slots = len(offset), len(offset[0])
    moved_refs, w_refs = refs[:slots], refs[slots : slots + cores]
    out_refs = refs[slots + cores : 2 * slots + cores]
    left = take_slots(offset, core_ref, own_ref, moved_refs)
    rows, part = own_ref.shape[0], w_refs[0].shape[1]
    for j in range(cores):
        product = jnp.dot(left, w_refs[j][...], preferred_element_type=F32).astype(BF16)
        for s in range(slots):
            out_refs[s][:, j * part : (j + 1) * part] = product[s * rows : (s + 1) * rows]


def project(place, own, moved, weights, offset):
    rows = own.shape[0]
    depth, part = weights[0].shape
    cores, slots = len(offset), len(offset[0])
    return pl.pallas_call(
        functools.partial(project_kernel, offset),
        out_shape=[jax.ShapeDtypeStruct((rows, part * cores), BF16)] * slots,
        in_specs=[SMEM, VMEM] + [VMEM] * (slots + cores),
        out_specs=[VMEM] * slots,
        compiler_params=pltpu.CompilerParams(vmem_limit_bytes=12 * MIB),
    )(place[1], own, *moved, *weights)


def norm_kernel(cores, experts, core_ref, *refs):
    sums_refs, stream_refs, gain_refs = refs[:cores], refs[cores : 2 * cores], refs[2 * cores : 3 * cores]
    ids_ref, routes_ref, mixed_ref, out_ref = refs[3 * cores :]
    rows, part = stream_refs[0].shape
    width = part * cores
    core = core_ref[0]
    squares = 0.0
    mixed = []
    for j in range(cores):
        block = from_natural(core, stream_refs[j][...].astype(F32), cores)
        for m in range(cores):
            other = sums_refs[m][:, (j ^ m) * part : ((j ^ m) + 1) * part]
            block = block + turned(other, m, cores)
        mixed.append(block)
        squares = squares + jnp.sum(block * block, axis=1, keepdims=True)
    mixed_ref[...] = mixed[0]
    scale = lax.rsqrt(squares / width + 1e-06)
    for j in range(cores):
        out_ref[:, j * part : (j + 1) * part] = (mixed[j] * scale * gain_refs[j][...]).astype(BF16)
    picks = ids_ref.shape[0]
    extra = out_ref.shape[1] - width
    ids, routes = ids_ref[...], routes_ref[...]
    shares = routes / jnp.sum(routes, axis=0, keepdims=True)
    line = lax.broadcasted_iota(jnp.int32, (extra, rows), 0)
    line = jnp.where(line < experts, line, line - experts)
    combine = jnp.zeros((extra, rows), F32)
    for k in range(picks):
        combine = jnp.where(ids[k : k + 1, :] == line, shares[k : k + 1, :], combine)
    combine = jnp.concatenate([combine, jnp.zeros((extra, 128 - rows), F32)], axis=1)
    combine = from_natural(core, jnp.transpose(combine)[:rows], cores)
    upper = combine.astype(BF16)
    lower = (combine - upper.astype(F32)).astype(BF16)
    lane = lax.broadcasted_iota(jnp.int32, (rows, extra), 1)
    out_ref[:, width:] = jnp.where(lane < experts, upper.astype(F32), lower.astype(F32)).astype(BF16)


def normalise(place, sums, stream, gain, ids, routes, experts):
    rows, part = stream[0].shape
    cores = len(sums)
    extra = -(-2 * experts // 128) * 128
    return pl.pallas_call(
        functools.partial(norm_kernel, cores, experts),
        out_shape=(
            jax.ShapeDtypeStruct((rows, part), F32),
            jax.ShapeDtypeStruct((rows, part * cores + extra), BF16),
        ),
        in_specs=[SMEM] + [VMEM] * (3 * cores + 2),
        out_specs=(VMEM, VMEM),
        compiler_params=pltpu.CompilerParams(vmem_limit_bytes=8 * MIB),
    )(place[1], *sums, *stream, *gain, ids.T, routes.T)


def fetch_kernel(count, *refs):
    sources, targets, sems = refs[:count], refs[count : 2 * count], refs[2 * count]
    copies = [
        pltpu.make_async_copy(sources[i].at[0], targets[i], sems.at[i]) for i in range(count)
    ]
    for copy in copies:
        copy.start()
    for copy in copies:
        copy.wait()


def fetch(weights):
    count = len(weights)
    return pl.pallas_call(
        functools.partial(fetch_kernel, count),
        out_shape=[jax.ShapeDtypeStruct(w.shape[1:], w.dtype) for w in weights],
        in_specs=[ANY] * count,
        out_specs=[VMEM] * count,
        scratch_shapes=[pltpu.SemaphoreType.DMA((count,))],
        compiler_params=pltpu.CompilerParams(vmem_limit_bytes=42 * MIB),
    )(*weights)


def expert_kernel(offset, devs, me_ref, core_ref, own_ref, *refs):
    cores, slots = len(offset), len(offset[0])
    moved_refs, refs = refs[:slots], refs[slots:]
    first_refs, refs = refs[: 3 * cores], refs[3 * cores :]
    weight_refs = refs[: 3 * cores]
    out_refs = refs[3 * cores : 3 * cores + slots]
    gate_buf, up_buf, down_buf, sems = refs[3 * cores + slots :]
    local, part, hidden = weight_refs[0].shape
    rows = own_ref.shape[0]
    width = part * cores
    bufs = (gate_buf, up_buf, down_buf)

    def copy(kind, j, e):
        return pltpu.make_async_copy(
            weight_refs[kind * cores + j].at[e], bufs[kind].at[j, e - 1], sems.at[kind, j, e - 1]
        )

    def weight(kind, j, e):
        if e == 0:
            return first_refs[kind * cores + j][...]
        copy(kind, j, e).wait()
        return bufs[kind][j, e - 1]

    for e in range(1, local):
        for kind in range(3):
            for j in range(cores):
                copy(kind, j, e).start()
    tokens = take_slots(offset, core_ref, own_ref, moved_refs)
    tail = tokens[:, width:].astype(F32)
    lane = lax.broadcasted_iota(jnp.int32, tail.shape, 1)
    experts = local * devs
    total = [0.0] * cores
    for e in range(local):
        mine = me_ref[0] * local + e
        share = jnp.sum(
            jnp.where((lane == mine) | (lane == mine + experts), tail, 0.0), axis=1, keepdims=True
        )
        sums = []
        for kind in range(2):
            value = 0.0
            for j in range(cores):
                value = value + jnp.dot(
                    tokens[:, j * part : (j + 1) * part],
                    weight(kind, j, e),
                    preferred_element_type=F32,
                )
            sums.append(value)
        gate, up = sums
        active = (gate / (1.0 + jnp.exp(-gate)) * up * share).astype(BF16)
        for j in range(cores):
            total[j] = total[j] + jnp.dot(active, weight(2, j, e), preferred_element_type=F32)
    for j in range(cores):
        for s in range(slots):
            out_refs[s][:, j * part : (j + 1) * part] = total[j][
                s * rows : (s + 1) * rows
            ].astype(BF16)


def apply_experts(place, own, moved, first, weights, offset, devs):
    cores, slots = len(offset), len(offset[0])
    local, part, hidden = weights[0].shape
    rows = own.shape[0]
    return pl.pallas_call(
        functools.partial(expert_kernel, offset, devs),
        out_shape=[jax.ShapeDtypeStruct((rows, part * cores), BF16)] * slots,
        in_specs=[SMEM, SMEM, VMEM] + [VMEM] * (slots + 3 * cores) + [ANY] * (3 * cores),
        out_specs=[VMEM] * slots,
        scratch_shapes=[
            pltpu.VMEM((cores, local - 1, part, hidden), BF16),
            pltpu.VMEM((cores, local - 1, part, hidden), BF16),
            pltpu.VMEM((cores, local - 1, hidden, part), BF16),
            pltpu.SemaphoreType.DMA((3, cores, local - 1)),
        ],
        compiler_params=pltpu.CompilerParams(vmem_limit_bytes=42 * MIB),
    )(*place, own, *moved, *first, *weights)


def per_device(
    query,
    stored_keys,
    stored_values,
    incoming_key,
    incoming_value,
    lengths,
    out_weight,
    residual,
    norm_gain,
    expert_ids,
    route_weights,
    w_gate,
    w_up,
    w_down,
):
    devs = lax.axis_size("dev")
    cores = lax.axis_size("pair")
    me = lax.axis_index("dev")
    core = lax.axis_index("pair")
    slots = devs // cores
    offset = TUNED.get(
        (devs, cores), [[c * slots + s for s in range(slots)] for c in range(cores)]
    )
    place = (me.astype(jnp.int32).reshape(1), core.astype(jnp.int32).reshape(1))
    rows, part = residual.shape
    barrier = lax.optimization_barrier

    def from_core(value, m):
        return lax.ppermute(value, "pair", [(c, c ^ m) for c in range(cores)])

    def gathered(value):
        return [value] + [from_core(value, m) for m in range(1, cores)]

    def swap(value, s):
        pairs = [
            (d * cores + c, (d ^ offset[c][s]) * cores + c)
            for d in range(devs)
            for c in range(cores)
            if offset[c][s]
        ]
        return lax.ppermute(value, ("dev", "pair"), pairs)

    own_slot = [[c for c in range(cores) if offset[c][s] == 0] for s in range(slots)]

    def total_of(own, moved):
        result = 0.0
        for s in (2, 3, 0, 1):
            block = moved[s]
            for c in own_slot[s]:
                block = jnp.where(core == c, own[s], block)
            result = result + block.astype(F32)
        return result

    def own_block(blocks):
        return blocks[[s for s in range(slots) if own_slot[s]][0]]

    stream = gathered(residual)
    gain = gathered(norm_gain.reshape(1, part))
    wg = gathered(w_gate)
    attended = attend(
        query, stored_keys, stored_values, incoming_key, incoming_value, lengths, place, offset
    )
    attended, wg, stream, gain = barrier((attended, wg, stream, gain))
    mine = barrier([attended[0][s] for s in range(slots)])
    theirs = [from_core(attended[m], m) for m in range(1, cores)]
    outgoing = [
        jnp.concatenate([mine[s]] + [block[s] for block in theirs], axis=0) for s in range(slots)
    ]
    outgoing, out_weight, w_up, w_down = barrier((outgoing, out_weight, w_up, w_down))
    wo = gathered(out_weight)
    arrived = [swap(outgoing[s], s) for s in range(slots)]
    arrived, wo, w_up, w_down = barrier((arrived, wo, w_up, w_down))
    wu = gathered(w_up)
    partial = project(place, own_block(outgoing), arrived, wo, offset)
    sums = total_of(partial, [swap(partial[s], s) for s in range(slots)])
    sums, wu, w_down = barrier((sums, wu, w_down))
    mixed, packed = normalise(
        place, gathered(sums), stream, gain, expert_ids, route_weights, w_gate.shape[0] * devs
    )
    packed, weights, w_down = barrier((packed, wg + wu, w_down))
    tokens = [swap(packed, s) for s in range(slots)]
    weights = weights + gathered(w_down)
    first = fetch(weights)
    produced = apply_experts(place, packed, tokens, first, weights, offset, devs)
    back = total_of(produced, [swap(produced[s], s) for s in range(slots)])
    result = mixed + back[:, :part]
    for m in range(1, cores):
        other = from_core(back[:, m * part : (m + 1) * part], m)
        result = result + turned(other, m, cores)
    return from_natural(core, result, cores).astype(BF16)


def solution(mesh):
    in_specs = (
        P(("groups", "dev", "pair"), None, None),
        P(("groups", "dev", "pair"), None, None, None),
        P(("groups", "dev", "pair"), None, None, None),
        P(("groups", "dev", "pair"), None, None),
        P(("groups", "dev", "pair"), None, None),
        P(("groups", "dev", "pair")),
        P("dev", "pair"),
        P(("groups", "dev"), "pair"),
        P("pair"),
        P(("groups", "dev"), None),
        P(("groups", "dev"), None),
        P("dev", "pair", None),
        P("dev", "pair", None),
        P("dev", None, "pair"),
    )
    out_specs = P(("groups", "dev"), "pair")
    return jax.shard_map(
        per_device, mesh=mesh, in_specs=in_specs, out_specs=out_specs, check_vma=False
    )
```

```python
import functools
import math

import jax
import jax.numpy as jnp
from jax import lax
from jax.experimental import pallas as pl
from jax.experimental.pallas import tpu as pltpu
from jax.sharding import PartitionSpec as P

F32 = jnp.float32
BF16 = jnp.bfloat16
VMEM = pl.BlockSpec(memory_space=pltpu.VMEM)
SMEM = pl.BlockSpec(memory_space=pltpu.SMEM)
ANY = pl.BlockSpec(memory_space=pl.ANY)
MIB = 1024 * 1024
TUNED = {(8, 2): ((5, 0, 3, 6), (7, 1, 4, 2))}


def choose(core, values):
    result = jnp.int32(values[0])
    for c in range(1, len(values)):
        result = jnp.where(core == c, jnp.int32(values[c]), result)
    return result


def turned(value, m, cores):
    band = value.shape[0] // cores
    pieces = [value[i * band : (i + 1) * band] for i in range(cores)]
    return jnp.concatenate([pieces[i ^ m] for i in range(cores)], axis=0) if m else value


def from_natural(core, value, cores):
    result = value
    for c in range(1, cores):
        result = jnp.where(core == c, turned(value, c, cores), result)
    return result


def attend_kernel(
    kv_heads, offset, len_ref, me_ref, core_ref, q_hbm, k_hbm, v_hbm, ik_hbm, iv_hbm, *refs
):
    cores, slots = len(offset), len(offset[0])
    out_refs = refs[:cores]
    q_ref, ik_ref, iv_ref, k_buf, v_buf, mask_ref, all_ref, order_ref, sems, small_sems = refs[cores:]
    rows, heads, size = q_ref.shape
    span = k_buf.shape[1]
    per = heads // kv_heads
    block = heads // (cores * slots)
    scale = size ** (-0.5) * math.log2(math.e)
    step = 4
    chunks = 4
    chunk = span // chunks

    small = [
        pltpu.make_async_copy(source, target, small_sems.at[n])
        for n, (source, target) in enumerate(
            ((q_hbm, q_ref), (ik_hbm, ik_ref), (iv_hbm, iv_ref))
        )
    ]
    for copy in small:
        copy.start()

    lengths = [len_ref[r] for r in range(rows)]
    ranks = [jnp.int32(0)] * rows
    for i in range(rows):
        for j in range(i + 1, rows):
            later = (lengths[i] < lengths[j]).astype(jnp.int32)
            ranks[i] = ranks[i] + later
            ranks[j] = ranks[j] + (1 - later)
    for r in range(rows):
        order_ref[ranks[r]] = jnp.int32(r)

    def copies(i, used):
        r = order_ref[i]
        part = pl.ds(0, used)
        return (
            pltpu.make_async_copy(k_hbm.at[r, part], k_buf.at[r, part], sems.at[0, i]),
            pltpu.make_async_copy(v_hbm.at[r, part], v_buf.at[r, part], sems.at[1, i]),
        )

    def by_length(i, work):
        needed = (len_ref[order_ref[i * step]] * kv_heads + (chunk - 1)) // chunk
        for n in range(1, chunks + 1):

            @pl.when(needed == n)
            def _():
                work(n * chunk)

    def begin(i, carry):
        def work(used):
            for j in range(step):
                for copy in copies(i * step + j, used):
                    copy.start()

        by_length(i, work)
        return carry

    lax.fori_loop(0, rows // step, begin, 0)
    column = lax.broadcasted_iota(jnp.int32, (heads, span), 1)
    head = lax.broadcasted_iota(jnp.int32, (heads, span), 0)
    mask_ref[...] = jnp.where((column & (kv_heads - 1)) == (head >> (per.bit_length() - 1)), column, 1 << 30)

    def spread(value):
        return jnp.concatenate(
            [
                jnp.broadcast_to(value[g : g + 1, :].astype(F32), (per, size))
                for g in range(kv_heads)
            ],
            axis=0,
        )

    def several(group, used):
        queries = [q_ref[r] for r in group]
        scores = [
            lax.dot_general(
                q, k_buf[r, :used], (((1,), (1,)), ((), ())), preferred_element_type=F32
            )
            for q, r in zip(queries, group)
        ]
        own = [
            jnp.sum(q.astype(F32) * spread(ik_ref[r]), axis=1, keepdims=True)
            for q, r in zip(queries, group)
        ]
        scores = [
            jnp.where(mask_ref[:, :used] < len_ref[r] * kv_heads, x, -1e30)
            for x, r in zip(scores, group)
        ]
        peak = [
            jnp.maximum(jnp.max(x, axis=1, keepdims=True), o) for x, o in zip(scores, own)
        ]
        expo = [jnp.exp2((x - p) * scale) for x, p in zip(scores, peak)]
        accum = [
            jnp.dot(x.astype(BF16), v_buf[r, :used], preferred_element_type=F32)
            for x, r in zip(expo, group)
        ]
        fresh = [jnp.exp2((o - p) * scale) for o, p in zip(own, peak)]
        total = [jnp.sum(x, axis=1, keepdims=True) + f for x, f in zip(expo, fresh)]
        for x, f, t, r in zip(accum, fresh, total, group):
            all_ref[pl.ds(r, heads, stride=rows), :] = (x + f * spread(iv_ref[r])) / t

    def body(i, carry):
        def work(used):
            for j in range(step):
                for copy in copies(i * step + j, used):
                    copy.wait()
            several([order_ref[i * step + j] for j in range(step)], used)

        by_length(i, work)
        return carry

    for copy in small:
        copy.wait()
    lax.fori_loop(0, rows // step, body, 0)
    me, core = me_ref[0], core_ref[0]
    for m in range(cores):
        for s in range(slots):
            which = me ^ choose(core, [offset[c ^ m][s] for c in range(cores)])
            for h in range(block):
                at = pl.multiple_of((which * block + h) * rows, rows)
                out_refs[m][s, :, h * size : (h + 1) * size] = all_ref[
                    pl.ds(at, rows), :
                ].astype(BF16)


def attend(query, keys, values, fresh_key, fresh_value, lengths, place, offset):
    rows, heads, size = query.shape
    positions, kv_heads = keys.shape[1:3]
    span = positions * kv_heads
    cores, slots = len(offset), len(offset[0])
    width = heads * size // (cores * slots)
    return pl.pallas_call(
        functools.partial(attend_kernel, kv_heads, offset),
        out_shape=[jax.ShapeDtypeStruct((slots, rows, width), BF16)] * cores,
        in_specs=[SMEM, SMEM, SMEM] + [ANY] * 5,
        out_specs=[VMEM] * cores,
        scratch_shapes=[
            pltpu.VMEM(query.shape, BF16),
            pltpu.VMEM(fresh_key.shape, BF16),
            pltpu.VMEM(fresh_value.shape, BF16),
            pltpu.VMEM((rows, span, size), BF16),
            pltpu.VMEM((rows, span, size), BF16),
            pltpu.VMEM((heads, span), jnp.int32),
            pltpu.VMEM((heads * rows, size), F32),
            pltpu.SMEM((rows,), jnp.int32),
            pltpu.SemaphoreType.DMA((2, rows)),
            pltpu.SemaphoreType.DMA((3,)),
        ],
        compiler_params=pltpu.CompilerParams(vmem_limit_bytes=60 * MIB),
    )(
        lengths,
        *place,
        query,
        keys.reshape(rows, span, size),
        values.reshape(rows, span, size),
        fresh_key,
        fresh_value,
    )


def take_slots(offset, core_ref, own_ref, moved_refs):
    core = core_ref[0]
    result = []
    for s, ref in enumerate(moved_refs):
        block = ref[...]
        for c in range(len(offset)):
            if offset[c][s] == 0:
                block = jnp.where(core == c, own_ref[...], block)
        result.append(block)
    return jnp.concatenate(result, axis=0)


def project_kernel(offset, core_ref, own_ref, *refs):
    cores, slots = len(offset), len(offset[0])
    moved_refs, w_refs = refs[:slots], refs[slots : slots + cores]
    out_refs = refs[slots + cores : 2 * slots + cores]
    left = take_slots(offset, core_ref, own_ref, moved_refs)
    rows, part = own_ref.shape[0], w_refs[0].shape[1]
    for j in range(cores):
        product = jnp.dot(left, w_refs[j][...], preferred_element_type=F32).astype(BF16)
        for s in range(slots):
            out_refs[s][:, j * part : (j + 1) * part] = product[s * rows : (s + 1) * rows]


def project(place, own, moved, weights, offset):
    rows = own.shape[0]
    depth, part = weights[0].shape
    cores, slots = len(offset), len(offset[0])
    return pl.pallas_call(
        functools.partial(project_kernel, offset),
        out_shape=[jax.ShapeDtypeStruct((rows, part * cores), BF16)] * slots,
        in_specs=[SMEM, VMEM] + [VMEM] * (slots + cores),
        out_specs=[VMEM] * slots,
        compiler_params=pltpu.CompilerParams(vmem_limit_bytes=12 * MIB),
    )(place[1], own, *moved, *weights)


def norm_kernel(cores, experts, core_ref, *refs):
    sums_refs, stream_refs, gain_refs = refs[:cores], refs[cores : 2 * cores], refs[2 * cores : 3 * cores]
    ids_ref, routes_ref, mixed_ref, out_ref = refs[3 * cores :]
    rows, part = stream_refs[0].shape
    width = part * cores
    core = core_ref[0]
    squares = 0.0
    mixed = []
    for j in range(cores):
        block = from_natural(core, stream_refs[j][...].astype(F32), cores)
        for m in range(cores):
            other = sums_refs[m][:, (j ^ m) * part : ((j ^ m) + 1) * part]
            block = block + turned(other, m, cores)
        mixed.append(block)
        squares = squares + jnp.sum(block * block, axis=1, keepdims=True)
    mixed_ref[...] = mixed[0]
    scale = lax.rsqrt(squares / width + 1e-06)
    for j in range(cores):
        out_ref[:, j * part : (j + 1) * part] = (mixed[j] * scale * gain_refs[j][...]).astype(BF16)
    picks = ids_ref.shape[0]
    extra = out_ref.shape[1] - width
    ids, routes = ids_ref[...], routes_ref[...]
    shares = routes / jnp.sum(routes, axis=0, keepdims=True)
    line = lax.broadcasted_iota(jnp.int32, (extra, rows), 0)
    line = jnp.where(line < experts, line, line - experts)
    combine = jnp.zeros((extra, rows), F32)
    for k in range(picks):
        combine = jnp.where(ids[k : k + 1, :] == line, shares[k : k + 1, :], combine)
    combine = jnp.concatenate([combine, jnp.zeros((extra, 128 - rows), F32)], axis=1)
    combine = from_natural(core, jnp.transpose(combine)[:rows], cores)
    upper = combine.astype(BF16)
    lower = (combine - upper.astype(F32)).astype(BF16)
    lane = lax.broadcasted_iota(jnp.int32, (rows, extra), 1)
    out_ref[:, width:] = jnp.where(lane < experts, upper.astype(F32), lower.astype(F32)).astype(BF16)


def normalise(place, sums, stream, gain, ids, routes, experts):
    rows, part = stream[0].shape
    cores = len(sums)
    extra = -(-2 * experts // 128) * 128
    return pl.pallas_call(
        functools.partial(norm_kernel, cores, experts),
        out_shape=(
            jax.ShapeDtypeStruct((rows, part), F32),
            jax.ShapeDtypeStruct((rows, part * cores + extra), BF16),
        ),
        in_specs=[SMEM] + [VMEM] * (3 * cores + 2),
        out_specs=(VMEM, VMEM),
        compiler_params=pltpu.CompilerParams(vmem_limit_bytes=8 * MIB),
    )(place[1], *sums, *stream, *gain, ids.T, routes.T)


def fetch_kernel(count, *refs):
    sources, targets, sems = refs[:count], refs[count : 2 * count], refs[2 * count]
    copies = [
        pltpu.make_async_copy(sources[i].at[0], targets[i], sems.at[i]) for i in range(count)
    ]
    for copy in copies:
        copy.start()
    for copy in copies:
        copy.wait()


def fetch(weights):
    count = len(weights)
    return pl.pallas_call(
        functools.partial(fetch_kernel, count),
        out_shape=[jax.ShapeDtypeStruct(w.shape[1:], w.dtype) for w in weights],
        in_specs=[ANY] * count,
        out_specs=[VMEM] * count,
        scratch_shapes=[pltpu.SemaphoreType.DMA((count,))],
        compiler_params=pltpu.CompilerParams(vmem_limit_bytes=42 * MIB),
    )(*weights)


def expert_kernel(offset, devs, me_ref, core_ref, own_ref, *refs):
    cores, slots = len(offset), len(offset[0])
    moved_refs, refs = refs[:slots], refs[slots:]
    first_refs, refs = refs[: 3 * cores], refs[3 * cores :]
    weight_refs = refs[: 3 * cores]
    out_refs = refs[3 * cores : 3 * cores + slots]
    gate_buf, up_buf, down_buf, sems = refs[3 * cores + slots :]
    local, part, hidden = weight_refs[0].shape
    rows = own_ref.shape[0]
    width = part * cores
    bufs = (gate_buf, up_buf, down_buf)

    def copy(kind, j, e):
        return pltpu.make_async_copy(
            weight_refs[kind * cores + j].at[e], bufs[kind].at[j, e - 1], sems.at[kind, j, e - 1]
        )

    def weight(kind, j, e):
        if e == 0:
            return first_refs[kind * cores + j][...]
        copy(kind, j, e).wait()
        return bufs[kind][j, e - 1]

    for e in range(1, local):
        for kind in range(3):
            for j in range(cores):
                copy(kind, j, e).start()
    tokens = take_slots(offset, core_ref, own_ref, moved_refs)
    tail = tokens[:, width:].astype(F32)
    lane = lax.broadcasted_iota(jnp.int32, tail.shape, 1)
    experts = local * devs
    total = [0.0] * cores
    for e in range(local):
        mine = me_ref[0] * local + e
        share = jnp.sum(
            jnp.where((lane == mine) | (lane == mine + experts), tail, 0.0), axis=1, keepdims=True
        )
        sums = []
        for kind in range(2):
            value = 0.0
            for j in range(cores):
                value = value + jnp.dot(
                    tokens[:, j * part : (j + 1) * part],
                    weight(kind, j, e),
                    preferred_element_type=F32,
                )
            sums.append(value)
        gate, up = sums
        active = (gate / (1.0 + jnp.exp(-gate)) * up * share).astype(BF16)
        for j in range(cores):
            total[j] = total[j] + jnp.dot(active, weight(2, j, e), preferred_element_type=F32)
    for j in range(cores):
        for s in range(slots):
            out_refs[s][:, j * part : (j + 1) * part] = total[j][
                s * rows : (s + 1) * rows
            ].astype(BF16)


def apply_experts(place, own, moved, first, weights, offset, devs):
    cores, slots = len(offset), len(offset[0])
    local, part, hidden = weights[0].shape
    rows = own.shape[0]
    return pl.pallas_call(
        functools.partial(expert_kernel, offset, devs),
        out_shape=[jax.ShapeDtypeStruct((rows, part * cores), BF16)] * slots,
        in_specs=[SMEM, SMEM, VMEM] + [VMEM] * (slots + 3 * cores) + [ANY] * (3 * cores),
        out_specs=[VMEM] * slots,
        scratch_shapes=[
            pltpu.VMEM((cores, local - 1, part, hidden), BF16),
            pltpu.VMEM((cores, local - 1, part, hidden), BF16),
            pltpu.VMEM((cores, local - 1, hidden, part), BF16),
            pltpu.SemaphoreType.DMA((3, cores, local - 1)),
        ],
        compiler_params=pltpu.CompilerParams(vmem_limit_bytes=42 * MIB),
    )(*place, own, *moved, *first, *weights)


def per_device(
    query,
    stored_keys,
    stored_values,
    incoming_key,
    incoming_value,
    lengths,
    out_weight,
    residual,
    norm_gain,
    expert_ids,
    route_weights,
    w_gate,
    w_up,
    w_down,
):
    devs = lax.axis_size("dev")
    cores = lax.axis_size("pair")
    me = lax.axis_index("dev")
    core = lax.axis_index("pair")
    slots = devs // cores
    offset = TUNED.get(
        (devs, cores), [[c * slots + s for s in range(slots)] for c in range(cores)]
    )
    place = (me.astype(jnp.int32).reshape(1), core.astype(jnp.int32).reshape(1))
    rows, part = residual.shape
    barrier = lax.optimization_barrier

    def from_core(value, m):
        return lax.ppermute(value, "pair", [(c, c ^ m) for c in range(cores)])

    def gathered(value):
        return [value] + [from_core(value, m) for m in range(1, cores)]

    def swap(value, s):
        pairs = [
            (d * cores + c, (d ^ offset[c][s]) * cores + c)
            for d in range(devs)
            for c in range(cores)
            if offset[c][s]
        ]
        return lax.ppermute(value, ("dev", "pair"), pairs)

    own_slot = [[c for c in range(cores) if offset[c][s] == 0] for s in range(slots)]

    def total_of(own, moved):
        result = 0.0
        for s in sorted(range(slots), key=lambda s: (s + slots // 2) % slots):
            block = moved[s]
            for c in own_slot[s]:
                block = jnp.where(core == c, own[s], block)
            result = result + block.astype(F32)
        return result

    def own_block(blocks):
        return blocks[[s for s in range(slots) if own_slot[s]][0]]

    stream = gathered(residual)
    gain = gathered(norm_gain.reshape(1, part))
    wg = gathered(w_gate)
    attended = attend(
        query, stored_keys, stored_values, incoming_key, incoming_value, lengths, place, offset
    )
    attended, wg, stream, gain = barrier((attended, wg, stream, gain))
    mine = barrier([attended[0][s] for s in range(slots)])
    theirs = [from_core(attended[m], m) for m in range(1, cores)]
    outgoing = [
        jnp.concatenate([mine[s]] + [block[s] for block in theirs], axis=0) for s in range(slots)
    ]
    outgoing, out_weight, w_up, w_down = barrier((outgoing, out_weight, w_up, w_down))
    wo = gathered(out_weight)
    arrived = [swap(outgoing[s], s) for s in range(slots)]
    arrived, wo, w_up, w_down = barrier((arrived, wo, w_up, w_down))
    wu = gathered(w_up)
    partial = project(place, own_block(outgoing), arrived, wo, offset)
    sums = total_of(partial, [swap(partial[s], s) for s in range(slots)])
    sums, wu, w_down = barrier((sums, wu, w_down))
    mixed, packed = normalise(
        place, gathered(sums), stream, gain, expert_ids, route_weights, w_gate.shape[0] * devs
    )
    packed, weights, w_down = barrier((packed, wg + wu, w_down))
    tokens = [swap(packed, s) for s in range(slots)]
    weights = weights + gathered(w_down)
    first = fetch(weights)
    produced = apply_experts(place, packed, tokens, first, weights, offset, devs)
    back = total_of(produced, [swap(produced[s], s) for s in range(slots)])
    result = mixed + back[:, :part]
    for m in range(1, cores):
        other = from_core(back[:, m * part : (m + 1) * part], m)
        result = result + turned(other, m, cores)
    return from_natural(core, result, cores).astype(BF16)


def solution(mesh):
    in_specs = (
        P(("groups", "dev", "pair"), None, None),
        P(("groups", "dev", "pair"), None, None, None),
        P(("groups", "dev", "pair"), None, None, None),
        P(("groups", "dev", "pair"), None, None),
        P(("groups", "dev", "pair"), None, None),
        P(("groups", "dev", "pair")),
        P("dev", "pair"),
        P(("groups", "dev"), "pair"),
        P("pair"),
        P(("groups", "dev"), None),
        P(("groups", "dev"), None),
        P("dev", "pair", None),
        P("dev", "pair", None),
        P("dev", None, "pair"),
    )
    out_specs = P(("groups", "dev"), "pair")
    return jax.shard_map(
        per_device, mesh=mesh, in_specs=in_specs, out_specs=out_specs, check_vma=False
    )
```

```python
import functools
import math

import jax
import jax.numpy as jnp
from jax import lax
from jax.experimental import pallas as pl
from jax.experimental.pallas import tpu as pltpu
from jax.sharding import PartitionSpec as P

F32 = jnp.float32
BF16 = jnp.bfloat16
VMEM = pl.BlockSpec(memory_space=pltpu.VMEM)
SMEM = pl.BlockSpec(memory_space=pltpu.SMEM)
ANY = pl.BlockSpec(memory_space=pl.ANY)
MIB = 1024 * 1024
TUNED = {(8, 2): ((5, 0, 3, 6), (7, 1, 4, 2))}


def choose(core, values):
    result = jnp.int32(values[0])
    for c in range(1, len(values)):
        result = jnp.where(core == c, jnp.int32(values[c]), result)
    return result


def turned(value, m, cores):
    band = value.shape[0] // cores
    pieces = [value[i * band : (i + 1) * band] for i in range(cores)]
    return jnp.concatenate([pieces[i ^ m] for i in range(cores)], axis=0) if m else value


def from_natural(core, value, cores):
    result = value
    for c in range(1, cores):
        result = jnp.where(core == c, turned(value, c, cores), result)
    return result


def attend_kernel(
    kv_heads, offset, len_ref, me_ref, core_ref, q_hbm, k_hbm, v_hbm, ik_hbm, iv_hbm, *refs
):
    cores, slots = len(offset), len(offset[0])
    out_refs = refs[:cores]
    q_ref, ik_ref, iv_ref, k_buf, v_buf, mask_ref, all_ref, order_ref, sems, small_sems = refs[cores:]
    rows, heads, size = q_ref.shape
    span = k_buf.shape[1]
    per = heads // kv_heads
    block = heads // (cores * slots)
    scale = size ** (-0.5) * math.log2(math.e)
    step = 4
    chunks = 4
    chunk = span // chunks

    small = [
        pltpu.make_async_copy(source, target, small_sems.at[n])
        for n, (source, target) in enumerate(
            ((q_hbm, q_ref), (ik_hbm, ik_ref), (iv_hbm, iv_ref))
        )
    ]
    for copy in small:
        copy.start()

    lengths = [len_ref[r] for r in range(rows)]
    ranks = [jnp.int32(0)] * rows
    for i in range(rows):
        for j in range(i + 1, rows):
            later = (lengths[i] < lengths[j]).astype(jnp.int32)
            ranks[i] = ranks[i] + later
            ranks[j] = ranks[j] + (1 - later)
    for r in range(rows):
        order_ref[ranks[r]] = jnp.int32(r)

    def copies(i, used):
        r = order_ref[i]
        part = pl.ds(0, used)
        return (
            pltpu.make_async_copy(k_hbm.at[r, part], k_buf.at[r, part], sems.at[0, i]),
            pltpu.make_async_copy(v_hbm.at[r, part], v_buf.at[r, part], sems.at[1, i]),
        )

    def by_length(i, work):
        needed = (len_ref[order_ref[i * step]] * kv_heads + (chunk - 1)) // chunk
        for n in range(1, chunks + 1):

            @pl.when(needed == n)
            def _():
                work(n * chunk)

    def begin(i, carry):
        def work(used):
            for j in range(step):
                for copy in copies(i * step + j, used):
                    copy.start()

        by_length(i, work)
        return carry

    lax.fori_loop(0, rows // step, begin, 0)
    column = lax.broadcasted_iota(jnp.int32, (heads, span), 1)
    head = lax.broadcasted_iota(jnp.int32, (heads, span), 0)
    mask_ref[...] = jnp.where((column & (kv_heads - 1)) == (head >> (per.bit_length() - 1)), column, 1 << 30)

    def spread(value):
        return jnp.concatenate(
            [
                jnp.broadcast_to(value[g : g + 1, :].astype(F32), (per, size))
                for g in range(kv_heads)
            ],
            axis=0,
        )

    def several(group, used):
        queries = [q_ref[r] for r in group]
        scores = [
            lax.dot_general(
                q, k_buf[r, :used], (((1,), (1,)), ((), ())), preferred_element_type=F32
            )
            for q, r in zip(queries, group)
        ]
        own = [
            jnp.sum(q.astype(F32) * spread(ik_ref[r]), axis=1, keepdims=True)
            for q, r in zip(queries, group)
        ]
        scores = [
            jnp.where(mask_ref[:, :used] < len_ref[r] * kv_heads, x, -1e30)
            for x, r in zip(scores, group)
        ]
        peak = [
            jnp.maximum(jnp.max(x, axis=1, keepdims=True), o) for x, o in zip(scores, own)
        ]
        expo = [jnp.exp2((x - p) * scale) for x, p in zip(scores, peak)]
        accum = [
            jnp.dot(x.astype(BF16), v_buf[r, :used], preferred_element_type=F32)
            for x, r in zip(expo, group)
        ]
        fresh = [jnp.exp2((o - p) * scale) for o, p in zip(own, peak)]
        total = [jnp.sum(x, axis=1, keepdims=True) + f for x, f in zip(expo, fresh)]
        for x, f, t, r in zip(accum, fresh, total, group):
            all_ref[pl.ds(r, heads, stride=rows), :] = (x + f * spread(iv_ref[r])) / t

    def body(i, carry):
        def work(used):
            for j in range(step):
                for copy in copies(i * step + j, used):
                    copy.wait()
            several([order_ref[i * step + j] for j in range(step)], used)

        by_length(i, work)
        return carry

    for copy in small:
        copy.wait()
    lax.fori_loop(0, rows // step, body, 0)
    me, core = me_ref[0], core_ref[0]
    for m in range(cores):
        for s in range(slots):
            which = me ^ choose(core, [offset[c ^ m][s] for c in range(cores)])
            for h in range(block):
                at = pl.multiple_of((which * block + h) * rows, rows)
                out_refs[m][s, :, h * size : (h + 1) * size] = all_ref[
                    pl.ds(at, rows), :
                ].astype(BF16)


def attend(query, keys, values, fresh_key, fresh_value, lengths, place, offset):
    rows, heads, size = query.shape
    positions, kv_heads = keys.shape[1:3]
    span = positions * kv_heads
    cores, slots = len(offset), len(offset[0])
    width = heads * size // (cores * slots)
    return pl.pallas_call(
        functools.partial(attend_kernel, kv_heads, offset),
        out_shape=[jax.ShapeDtypeStruct((slots, rows, width), BF16)] * cores,
        in_specs=[SMEM, SMEM, SMEM] + [ANY] * 5,
        out_specs=[VMEM] * cores,
        scratch_shapes=[
            pltpu.VMEM(query.shape, BF16),
            pltpu.VMEM(fresh_key.shape, BF16),
            pltpu.VMEM(fresh_value.shape, BF16),
            pltpu.VMEM((rows, span, size), BF16),
            pltpu.VMEM((rows, span, size), BF16),
            pltpu.VMEM((heads, span), jnp.int32),
            pltpu.VMEM((heads * rows, size), F32),
            pltpu.SMEM((rows,), jnp.int32),
            pltpu.SemaphoreType.DMA((2, rows)),
            pltpu.SemaphoreType.DMA((3,)),
        ],
        compiler_params=pltpu.CompilerParams(vmem_limit_bytes=60 * MIB),
    )(
        lengths,
        *place,
        query,
        keys.reshape(rows, span, size),
        values.reshape(rows, span, size),
        fresh_key,
        fresh_value,
    )


def take_slots(offset, core_ref, own_ref, moved_refs):
    core = core_ref[0]
    result = []
    for s, ref in enumerate(moved_refs):
        block = ref[...]
        for c in range(len(offset)):
            if offset[c][s] == 0:
                block = jnp.where(core == c, own_ref[...], block)
        result.append(block)
    return jnp.concatenate(result, axis=0)


def project_kernel(offset, core_ref, own_ref, *refs):
    cores, slots = len(offset), len(offset[0])
    moved_refs, w_refs = refs[:slots], refs[slots : slots + cores]
    out_refs = refs[slots + cores : 2 * slots + cores]
    left = take_slots(offset, core_ref, own_ref, moved_refs)
    rows, part = own_ref.shape[0], w_refs[0].shape[1]
    for j in range(cores):
        product = jnp.dot(left, w_refs[j][...], preferred_element_type=F32).astype(BF16)
        for s in range(slots):
            out_refs[s][:, j * part : (j + 1) * part] = product[s * rows : (s + 1) * rows]


def project(place, own, moved, weights, offset):
    rows = own.shape[0]
    depth, part = weights[0].shape
    cores, slots = len(offset), len(offset[0])
    return pl.pallas_call(
        functools.partial(project_kernel, offset),
        out_shape=[jax.ShapeDtypeStruct((rows, part * cores), BF16)] * slots,
        in_specs=[SMEM, VMEM] + [VMEM] * (slots + cores),
        out_specs=[VMEM] * slots,
        compiler_params=pltpu.CompilerParams(vmem_limit_bytes=12 * MIB),
    )(place[1], own, *moved, *weights)


def norm_kernel(cores, experts, core_ref, *refs):
    sums_refs, stream_refs, gain_refs = refs[:cores], refs[cores : 2 * cores], refs[2 * cores : 3 * cores]
    ids_ref, routes_ref, mixed_ref, out_ref = refs[3 * cores :]
    rows, part = stream_refs[0].shape
    width = part * cores
    core = core_ref[0]
    squares = 0.0
    mixed = []
    for j in range(cores):
        block = from_natural(core, stream_refs[j][...].astype(F32), cores)
        for m in range(cores):
            other = sums_refs[m][:, (j ^ m) * part : ((j ^ m) + 1) * part]
            block = block + turned(other, m, cores)
        mixed.append(block)
        squares = squares + jnp.sum(block * block, axis=1, keepdims=True)
    mixed_ref[...] = mixed[0]
    scale = lax.rsqrt(squares / width + 1e-06)
    for j in range(cores):
        out_ref[:, j * part : (j + 1) * part] = (mixed[j] * scale * gain_refs[j][...]).astype(BF16)
    picks = ids_ref.shape[0]
    extra = out_ref.shape[1] - width
    ids, routes = ids_ref[...], routes_ref[...]
    shares = routes / jnp.sum(routes, axis=0, keepdims=True)
    line = lax.broadcasted_iota(jnp.int32, (extra, rows), 0)
    line = jnp.where(line < experts, line, line - experts)
    combine = jnp.zeros((extra, rows), F32)
    for k in range(picks):
        combine = jnp.where(ids[k : k + 1, :] == line, shares[k : k + 1, :], combine)
    combine = jnp.concatenate([combine, jnp.zeros((extra, 128 - rows), F32)], axis=1)
    combine = from_natural(core, jnp.transpose(combine)[:rows], cores)
    upper = combine.astype(BF16)
    lower = (combine - upper.astype(F32)).astype(BF16)
    lane = lax.broadcasted_iota(jnp.int32, (rows, extra), 1)
    out_ref[:, width:] = jnp.where(lane < experts, upper.astype(F32), lower.astype(F32)).astype(BF16)


def normalise(place, sums, stream, gain, ids, routes, experts):
    rows, part = stream[0].shape
    cores = len(sums)
    extra = -(-2 * experts // 128) * 128
    return pl.pallas_call(
        functools.partial(norm_kernel, cores, experts),
        out_shape=(
            jax.ShapeDtypeStruct((rows, part), F32),
            jax.ShapeDtypeStruct((rows, part * cores + extra), BF16),
        ),
        in_specs=[SMEM] + [VMEM] * (3 * cores + 2),
        out_specs=(VMEM, VMEM),
        compiler_params=pltpu.CompilerParams(vmem_limit_bytes=8 * MIB),
    )(place[1], *sums, *stream, *gain, ids.T, routes.T)


def fetch_kernel(count, *refs):
    sources, targets, sems = refs[:count], refs[count : 2 * count], refs[2 * count]
    copies = [
        pltpu.make_async_copy(sources[i].at[0], targets[i], sems.at[i]) for i in range(count)
    ]
    for copy in copies:
        copy.start()
    for copy in copies:
        copy.wait()


def fetch(weights):
    count = len(weights)
    return pl.pallas_call(
        functools.partial(fetch_kernel, count),
        out_shape=[jax.ShapeDtypeStruct(w.shape[1:], w.dtype) for w in weights],
        in_specs=[ANY] * count,
        out_specs=[VMEM] * count,
        scratch_shapes=[pltpu.SemaphoreType.DMA((count,))],
        compiler_params=pltpu.CompilerParams(vmem_limit_bytes=42 * MIB),
    )(*weights)


def expert_kernel(offset, devs, me_ref, core_ref, own_ref, *refs):
    cores, slots = len(offset), len(offset[0])
    moved_refs, refs = refs[:slots], refs[slots:]
    first_refs, refs = refs[: 3 * cores], refs[3 * cores :]
    weight_refs = refs[: 3 * cores]
    out_refs = refs[3 * cores : 3 * cores + slots]
    gate_buf, up_buf, down_buf, sems = refs[3 * cores + slots :]
    local, part, hidden = weight_refs[0].shape
    rows = own_ref.shape[0]
    width = part * cores
    bufs = (gate_buf, up_buf, down_buf)

    def copy(kind, j, e):
        return pltpu.make_async_copy(
            weight_refs[kind * cores + j].at[e], bufs[kind].at[j, e - 1], sems.at[kind, j, e - 1]
        )

    def weight(kind, j, e):
        if e == 0:
            return first_refs[kind * cores + j][...]
        copy(kind, j, e).wait()
        return bufs[kind][j, e - 1]

    for e in range(1, local):
        for kind in range(3):
            for j in range(cores):
                copy(kind, j, e).start()
    tokens = take_slots(offset, core_ref, own_ref, moved_refs)
    tail = tokens[:, width:].astype(F32)
    lane = lax.broadcasted_iota(jnp.int32, tail.shape, 1)
    experts = local * devs
    total = [0.0] * cores
    for e in range(local):
        mine = me_ref[0] * local + e
        share = jnp.sum(
            jnp.where((lane == mine) | (lane == mine + experts), tail, 0.0), axis=1, keepdims=True
        )
        sums = []
        for kind in range(2):
            value = 0.0
            for j in range(cores):
                value = value + jnp.dot(
                    tokens[:, j * part : (j + 1) * part],
                    weight(kind, j, e),
                    preferred_element_type=F32,
                )
            sums.append(value)
        gate, up = sums
        active = (gate / (1.0 + jnp.exp(-gate)) * up * share).astype(BF16)
        for j in range(cores):
            total[j] = total[j] + jnp.dot(active, weight(2, j, e), preferred_element_type=F32)
    for j in range(cores):
        for s in range(slots):
            out_refs[s][:, j * part : (j + 1) * part] = total[j][
                s * rows : (s + 1) * rows
            ].astype(BF16)


def apply_experts(place, own, moved, first, weights, offset, devs):
    cores, slots = len(offset), len(offset[0])
    local, part, hidden = weights[0].shape
    rows = own.shape[0]
    return pl.pallas_call(
        functools.partial(expert_kernel, offset, devs),
        out_shape=[jax.ShapeDtypeStruct((rows, part * cores), BF16)] * slots,
        in_specs=[SMEM, SMEM, VMEM] + [VMEM] * (slots + 3 * cores) + [ANY] * (3 * cores),
        out_specs=[VMEM] * slots,
        scratch_shapes=[
            pltpu.VMEM((cores, local - 1, part, hidden), BF16),
            pltpu.VMEM((cores, local - 1, part, hidden), BF16),
            pltpu.VMEM((cores, local - 1, hidden, part), BF16),
            pltpu.SemaphoreType.DMA((3, cores, local - 1)),
        ],
        compiler_params=pltpu.CompilerParams(vmem_limit_bytes=42 * MIB),
    )(*place, own, *moved, *first, *weights)


def per_device(
    query,
    stored_keys,
    stored_values,
    incoming_key,
    incoming_value,
    lengths,
    out_weight,
    residual,
    norm_gain,
    expert_ids,
    route_weights,
    w_gate,
    w_up,
    w_down,
):
    devs = lax.axis_size("dev")
    cores = lax.axis_size("pair")
    me = lax.axis_index("dev")
    core = lax.axis_index("pair")
    slots = devs // cores
    offset = TUNED.get(
        (devs, cores), [[c * slots + s for s in range(slots)] for c in range(cores)]
    )
    place = (me.astype(jnp.int32).reshape(1), core.astype(jnp.int32).reshape(1))
    rows, part = residual.shape
    barrier = lax.optimization_barrier

    def from_core(value, m):
        return lax.ppermute(value, "pair", [(c, c ^ m) for c in range(cores)])

    def gathered(value):
        return [value] + [from_core(value, m) for m in range(1, cores)]

    def swap(value, s):
        pairs = [
            (d * cores + c, (d ^ offset[c][s]) * cores + c)
            for d in range(devs)
            for c in range(cores)
            if offset[c][s]
        ]
        return lax.ppermute(value, ("dev", "pair"), pairs)

    own_slot = [[c for c in range(cores) if offset[c][s] == 0] for s in range(slots)]

    def total_of(own, moved):
        result = 0.0
        for s in reversed(range(slots)):
            block = moved[s]
            for c in own_slot[s]:
                block = jnp.where(core == c, own[s], block)
            result = result + block.astype(F32)
        return result

    def own_block(blocks):
        return blocks[[s for s in range(slots) if own_slot[s]][0]]

    stream = gathered(residual)
    gain = gathered(norm_gain.reshape(1, part))
    wg = gathered(w_gate)
    attended = attend(
        query, stored_keys, stored_values, incoming_key, incoming_value, lengths, place, offset
    )
    attended, wg, stream, gain = barrier((attended, wg, stream, gain))
    mine = barrier([attended[0][s] for s in range(slots)])
    theirs = [from_core(attended[m], m) for m in range(1, cores)]
    outgoing = [
        jnp.concatenate([mine[s]] + [block[s] for block in theirs], axis=0) for s in range(slots)
    ]
    outgoing, out_weight, w_up, w_down = barrier((outgoing, out_weight, w_up, w_down))
    wo = gathered(out_weight)
    arrived = [swap(outgoing[s], s) for s in range(slots)]
    arrived, wo, w_up, w_down = barrier((arrived, wo, w_up, w_down))
    wu = gathered(w_up)
    partial = project(place, own_block(outgoing), arrived, wo, offset)
    sums = total_of(partial, [swap(partial[s], s) for s in range(slots)])
    sums, wu, w_down = barrier((sums, wu, w_down))
    mixed, packed = normalise(
        place, gathered(sums), stream, gain, expert_ids, route_weights, w_gate.shape[0] * devs
    )
    packed, weights, w_down = barrier((packed, wg + wu, w_down))
    tokens = [swap(packed, s) for s in range(slots)]
    weights = weights + gathered(w_down)
    first = fetch(weights)
    produced = apply_experts(place, packed, tokens, first, weights, offset, devs)
    back = total_of(produced, [swap(produced[s], s) for s in range(slots)])
    result = mixed + back[:, :part]
    for m in range(1, cores):
        other = from_core(back[:, m * part : (m + 1) * part], m)
        result = result + turned(other, m, cores)
    return from_natural(core, result, cores).astype(BF16)


def solution(mesh):
    in_specs = (
        P(("groups", "dev", "pair"), None, None),
        P(("groups", "dev", "pair"), None, None, None),
        P(("groups", "dev", "pair"), None, None, None),
        P(("groups", "dev", "pair"), None, None),
        P(("groups", "dev", "pair"), None, None),
        P(("groups", "dev", "pair")),
        P("dev", "pair"),
        P(("groups", "dev"), "pair"),
        P("pair"),
        P(("groups", "dev"), None),
        P(("groups", "dev"), None),
        P("dev", "pair", None),
        P("dev", "pair", None),
        P("dev", None, "pair"),
    )
    out_specs = P(("groups", "dev"), "pair")
    return jax.shard_map(
        per_device, mesh=mesh, in_specs=in_specs, out_specs=out_specs, check_vma=False
    )
```
